32 devices in a mesh: pb: 2 (over y), pool: 4 (over z), ga: 2 (over x), pert: 2 (over core).
Axes of the slice: x: 2, y: 2, z: 4, core: 2. Of those that a mesh axis runs over, the one named last changes fastest.
Arguments:
- wavefunctions: bfloat16 [64, 12, 240, 128], P('pool', 'ga'), may hold values from -6 to 6
- potentials: float32 [12, 12, 240], P(('pb', 'pert'), 'ga'), parts along dimension 0, may hold values from -6 to 6
- pert_order: int32 [6], replicated, may hold values from 0 to 5, each once
- partners: int32 [128], P('pb'), parts along dimension 0, may hold values from 0 to 63, as said below
Outputs:
- couplings: bfloat16 [128, 6, 2, 128, 128], P(('pb', 'pool'), 'pert', None, 'ga'), parts along dimension 0
The draws below stay inside these ranges and needn't reach their ends.
There are 2 independent parts, one for each index of `pb`. The reference program is written for one: setup_inputs(seed, part) draws one part's arguments, and reference() takes and returns one part's arrays. A program takes and returns all parts, laid end to end along the dimension named above; an argument that names none is the same for every part. Nothing has to cross between parts.
Inputs may be any that keep to these rules, and one draw needn't show every extreme that they name: `partners`: A permutation of the 64 k-points; k-point k is owned by pool k // 16. For any two pools (one pool with itself included), at most 5 k-points of the one have their k+q owned by the other, and exactly 5 for some pair in every draw. The numbers of k-points that one pool takes from each pool are the same list for every pool, up to order. `pert_order`: each number once.
All inputs are finite; a program needn't handle non-finite values.
Results may differ from the reference program's by a relative error of at most 0.0073.
Values may be sent and summed in bfloat16 or wider, within the bound.
No kernel may reach another device: no remote copies, remote signals or barrier semaphores. Data moves between devices by JAX's collectives and lax.ppermute only.
A program may use at most 128 MiB of HBM per device.

```python
import math
import jax
import jax.numpy as jnp
from jax import lax

BANDS = 128
ZGRID = 120
PERTS = 6
K_DEV = 16
KPOINTS = 64
ALL_COLUMNS = 12
CAP = 5
N_POOL = 4


def draw_partners(key, part):
    key = jax.random.fold_in(key, 7)
    pick_key, score_key, label_key, hold_key, need_key = jax.random.split(key, 5)
    slot_total = N_POOL * CAP
    favored = jax.random.randint(pick_key, (), 0, N_POOL)
    scores = jax.random.permutation(score_key, slot_total).astype(jnp.int32)
    offsets_all = jnp.arange(slot_total, dtype=jnp.int32) // CAP
    scores = jnp.where(offsets_all == favored, scores - slot_total, scores)
    ordering = jnp.argsort(scores)
    offsets = jnp.sort(offsets_all[ordering[:K_DEV]])
    labels = jax.random.permutation(label_key, N_POOL).astype(jnp.int32)
    unlabel = jnp.argsort(labels).astype(jnp.int32)
    target = unlabel[(labels[:, None] + offsets[None, :]) % N_POOL]
    need_perm = jax.vmap(lambda sub_key: jax.random.permutation(sub_key, K_DEV))(jax.random.split(need_key, N_POOL)).astype(jnp.int32)
    hold_perm = jax.vmap(lambda sub_key: jax.random.permutation(sub_key, K_DEV))(jax.random.split(hold_key, N_POOL)).astype(jnp.int32)
    slot_range = jnp.arange(K_DEV, dtype=jnp.int32)
    partner_ids = target * K_DEV + hold_perm[target, slot_range[None, :]]
    where_k = jnp.arange(N_POOL, dtype=jnp.int32)[:, None] * K_DEV + need_perm
    return jnp.zeros((KPOINTS,), jnp.int32).at[where_k.reshape(-1)].set(partner_ids.reshape(-1))


def level_of(rng, extent, cuts, smallest, largest):
    level, own = 1.0, jax.random.fold_in(rng, 6)
    for dim, parts in cuts:
        heights = jnp.exp(jax.random.uniform(jax.random.fold_in(own, dim), (parts,), jnp.float32, smallest / len(cuts), largest / len(cuts)))
        level = level * jnp.repeat(heights, extent[dim] // parts).reshape([-1 if axis == dim else 1 for axis in range(len(extent))])
    return level


def noise(rng, shape, scale, limit, cuts=(), kind=jnp.bfloat16):
    entries = jax.random.normal(rng, shape, jnp.float32) * scale
    if len(cuts) > 0:
        entries = level_of(rng, shape, cuts, -0.22, 0.18) * entries
    return jnp.clip(entries, min=-limit, max=limit).astype(kind)


def setup_inputs(seed: int = 0, part: int = 0) -> dict:
    streams_of = jax.random.split(jax.random.key(seed), 5)
    own_keys = jax.random.split(jax.random.fold_in(streams_of[4], part), 5)
    return {
        "wavefunctions": noise(streams_of[0], (KPOINTS, ALL_COLUMNS, 2 * ZGRID, BANDS), 1.0, 6.0, ((0, 4), (1, 2))),
        "potentials": noise(own_keys[1], (PERTS, ALL_COLUMNS, 2 * ZGRID), 1.0, 6.0, ((0, 2), (1, 2)), jnp.float32),
        "pert_order": jax.random.permutation(streams_of[2], PERTS).astype(jnp.int32),
        "partners": draw_partners(jax.random.fold_in(jax.random.fold_in(streams_of[4], part), 71), part),
    }


def dft_table(length):
    positions = jnp.arange(length, dtype=jnp.int32)
    product = positions[:, None] * positions[None, :] % length
    angles = product.astype(jnp.float32) * (2.0 * math.pi / length)
    cosine = jnp.cos(angles) / math.sqrt(length)
    sine_part = jnp.sin(angles) / math.sqrt(length)
    upper_rows = jnp.concatenate([cosine, -sine_part], axis=1)
    bottom = jnp.concatenate([sine_part, cosine], axis=1)
    return jnp.concatenate([upper_rows, bottom], axis=0).astype(jnp.bfloat16)

def to_real(blocks, lookup_table):
    return jnp.einsum('zg,cgn->czn', lookup_table.astype(jnp.float32), blocks.astype(jnp.float32), precision=lax.Precision.HIGHEST).astype(jnp.bfloat16)

def couple(own_real, other_real, chosen, z_points):
    own_re = own_real[:, :z_points, :].astype(jnp.float32)
    own_im = own_real[:, z_points:, :].astype(jnp.float32)
    pot_re = chosen[:, :z_points, None]
    pot_im = chosen[:, z_points:, None]
    weighted_re = pot_re * own_re - pot_im * own_im
    weighted_im = pot_re * own_im + pot_im * own_re
    weighted = jnp.concatenate([weighted_re, weighted_im], axis=1).astype(jnp.bfloat16)
    turned = jnp.concatenate([weighted_im, -weighted_re], axis=1).astype(jnp.bfloat16)
    other_wide = other_real.astype(jnp.float32)
    real_part = jnp.einsum('csm,csn->mn', other_wide, weighted.astype(jnp.float32), precision=lax.Precision.HIGHEST)
    imag_part = jnp.einsum('csm,csn->mn', other_wide, turned.astype(jnp.float32), precision=lax.Precision.HIGHEST)
    return jnp.stack([real_part, imag_part], axis=0)

def reference(wavefunctions, potentials, pert_order, partners):
    lookup_table = dft_table(ZGRID)
    scaling = 1.0 / math.sqrt(ALL_COLUMNS * ZGRID)
    chosen_all = jnp.take(potentials, pert_order, axis=0)

    def one_point(kpoint):
        own_block = lax.dynamic_index_in_dim(wavefunctions, kpoint, 0, keepdims=False)
        partner_id = lax.dynamic_index_in_dim(partners, kpoint, 0, keepdims=False).astype(jnp.int32)
        other_block = lax.dynamic_index_in_dim(wavefunctions, partner_id, 0, keepdims=False)
        own_real = to_real(own_block, lookup_table)
        other_real = to_real(other_block, lookup_table)
        pieces = [couple(own_real, other_real, chosen_all[slot_index], ZGRID) for slot_index in range(PERTS)]
        return (jnp.stack(pieces, axis=0) * scaling).astype(jnp.bfloat16)
    return lax.map(one_point, jnp.arange(KPOINTS, dtype=jnp.int32))
```

```python
import functools
import math

import jax
import jax.numpy as jnp
from jax import lax
from jax.experimental import pallas as pl
from jax.experimental.pallas import tpu as pltpu
from jax.sharding import PartitionSpec as P

BF16 = jnp.bfloat16
F32 = jnp.float32
ANY = pl.BlockSpec(memory_space=pl.ANY)
SMEM = pl.BlockSpec(memory_space=pltpu.SMEM)
VMEM_LIMIT = 48 * 1024 * 1024


def dft_table(length):
    positions = jnp.arange(length, dtype=jnp.int32)
    product = positions[:, None] * positions[None, :] % length
    angles = product.astype(F32) * (2.0 * math.pi / length)
    cosine = jnp.cos(angles) / math.sqrt(length)
    sine_part = jnp.sin(angles) / math.sqrt(length)
    upper_rows = jnp.concatenate([cosine, -sine_part], axis=1)
    bottom = jnp.concatenate([sine_part, cosine], axis=1)
    return jnp.concatenate([upper_rows, bottom], axis=0).astype(BF16)


def plan_kernel(pools, local_k, cap, ids, partners, waves, plan, *rest):
    sends, sems = rest[:-1], rest[-1]
    me, core = ids[0], ids[1]
    places, counts = pools * cap, 2 * pools * cap

    def clear(i, carry):
        plan[i] = 0
        return carry

    lax.fori_loop(0, counts + 2 * pools, clear, 0)

    for shift in range(1, pools):
        taker = lax.rem(me + shift, pools)
        tally = counts + pools + shift

        def give(t, carry, shift=shift, taker=taker, tally=tally):
            want = partners[taker * local_k + t]

            @pl.when(lax.div(want, local_k) == me)
            def _():
                slot = plan[tally]
                pltpu.make_async_copy(
                    waves.at[lax.rem(want, local_k) * 2 + core],
                    sends[shift - 1].at[slot],
                    sems.at[shift - 1, slot],
                ).start()
                plan[tally] = slot + 1

            return carry

        lax.fori_loop(0, local_k, give, 0)

    def need(t, carry):
        want = partners[me * local_k + t]
        holder = lax.div(want, local_k)
        shift = lax.rem(me - holder + pools, pools)
        slot = plan[counts + shift]
        plan[shift * cap + slot] = t
        plan[places + shift * cap + slot] = want - holder * local_k
        plan[counts + shift] = slot + 1
        return carry

    lax.fori_loop(0, local_k, need, 0)

    for shift in range(1, pools):
        for slot in range(cap):

            @pl.when(slot < plan[counts + pools + shift])
            def _(shift=shift, slot=slot):
                pltpu.make_async_copy(
                    waves.at[0], sends[shift - 1].at[slot], sems.at[shift - 1, slot]
                ).wait()


def make_plan(ids, partners, waves, pools, local_k, cap):
    shape = (cap,) + waves.shape[1:]
    out = pl.pallas_call(
        functools.partial(plan_kernel, pools, local_k, cap),
        out_shape=[jax.ShapeDtypeStruct((2 * pools * cap + 2 * pools,), jnp.int32)]
        + [jax.ShapeDtypeStruct(shape, waves.dtype)] * (pools - 1),
        in_specs=[SMEM, SMEM, ANY],
        out_specs=[SMEM] + [ANY] * (pools - 1),
        scratch_shapes=[pltpu.SemaphoreType.DMA((pools - 1, cap))],
        name="plan_and_pick",
    )(ids, partners, waves)
    return out[0], out[1:]


def to_real(first, second, table, z_points):
    stacked = 2 * z_points
    cols = []
    for half in (first, second):
        for c in range(half.shape[0] // stacked):
            cols.append(half[c * stacked : (c + 1) * stacked])
    re, im = [], []
    for c in range(0, len(cols), 2):
        pair = jnp.concatenate(cols[c : c + 2], axis=1)
        out = jnp.dot(table, pair, preferred_element_type=F32)
        bands = pair.shape[1] // 2
        for side in range(2):
            lanes = slice(side * bands, (side + 1) * bands)
            re.append(out[:z_points, lanes])
            im.append(out[z_points:, lanes])
    return jnp.concatenate(re, axis=0).astype(BF16), jnp.concatenate(im, axis=0).astype(BF16)


def couple_kernel(pools, cap, shift, groups, z_points, scaling, plan, ids, table, pots,
                  own_a, own_b, other_a, other_b, keep, *rest):
    sends, whole = rest[:-1], rest[-1]
    slot = pl.program_id(0)
    my_group = ids[2]

    @pl.when(slot < plan[2 * pools * cap + shift])
    def _():
        lookup = table[...]
        own_re, own_im = to_real(own_a[0], own_b[0], lookup, z_points)
        u_re, u_im = own_re.astype(F32), own_im.astype(F32)
        o_re, o_im = to_real(other_a[0], other_b[0], lookup, z_points)
        other = jnp.concatenate([o_re, o_im], axis=1)
        bands = o_re.shape[1]
        share = bands // groups
        for j in range(pots.shape[0]):
            p_re, p_im = pots[j, 0], pots[j, 1]
            w_re = (p_re * u_re - p_im * u_im).astype(BF16)
            w_im = (p_re * u_im + p_im * u_re).astype(BF16)
            both = lax.dot_general(
                other, jnp.concatenate([w_re, w_im], axis=1),
                (((0,), (0,)), ((), ())), preferred_element_type=F32,
            )
            whole[2 * j] = (both[:bands, :bands] + both[bands:, bands:]) * scaling
            whole[2 * j + 1] = (both[:bands, bands:] - both[bands:, :bands]) * scaling
        for step in range(groups):
            start = pl.multiple_of(lax.rem(my_group + step, groups) * share, share)
            for part in range(2 * pots.shape[0]):
                block = whole[part, pl.ds(start, share), :]
                if step == 0:
                    keep[0, part] = block
                else:
                    sends[step - 1][0, part] = block.astype(BF16)


def couple(plan, ids, table, pots, waves, other_a, other_b, shift, pools, cap, groups, scaling):
    half, bands = waves.shape[1:]
    z_points = table.shape[0] // 2
    parts = 2 * pots.shape[0]
    share = bands // groups
    places = pools * cap
    block = (1, half, bands)

    def own(side):
        def where(i, plan, ids):
            core = ids[1] if side == 0 else 1 - ids[1]
            return plan[shift * cap + i] * 2 + core, 0, 0
        return pl.BlockSpec(block, where)

    def partner(side):
        def local(i, plan, ids):
            core = ids[1] if side == 0 else 1 - ids[1]
            return plan[places + i] * 2 + core, 0, 0

        def arrived(i, plan, ids):
            return i, 0, 0
        return pl.BlockSpec(block, local if shift == 0 else arrived)

    out_block = pl.BlockSpec((1, parts, share, bands), lambda i, plan, ids: (i, 0, 0, 0))
    rows = 2 * half // 2
    flops = cap * 2 * (parts // 2 * 4 * bands * bands * rows + 4 * half * 2 * z_points * bands)
    out = pl.pallas_call(
        functools.partial(couple_kernel, pools, cap, shift, groups, z_points, scaling),
        grid_spec=pltpu.PrefetchScalarGridSpec(
            num_scalar_prefetch=2,
            grid=(cap,),
            in_specs=[
                pl.BlockSpec(table.shape, lambda i, plan, ids: (0, 0)),
                pl.BlockSpec(pots.shape, lambda i, plan, ids: (0, 0, 0, 0)),
                own(0), own(1), partner(0), partner(1),
            ],
            out_specs=[out_block] * groups,
            scratch_shapes=[pltpu.VMEM((parts, bands, bands), F32)],
        ),
        out_shape=[jax.ShapeDtypeStruct((cap, parts, share, bands), F32)]
        + [jax.ShapeDtypeStruct((cap, parts, share, bands), BF16)] * (groups - 1),
        compiler_params=pltpu.CompilerParams(vmem_limit_bytes=VMEM_LIMIT),
        cost_estimate=pl.CostEstimate(
            flops=flops * 2, bytes_accessed=cap * 8 * half * bands, transcendentals=0
        ),
        name="couple",
    )(plan, ids, table, pots, waves, waves, other_a, other_b)
    return out[0], out[1:]


def combine_kernel(pools, cap, shift, terms, plan, *refs):
    result, stage, sems = refs[-3:]
    kept, arrived = refs[-4 - terms], refs[-3 - terms : -3]
    slot = pl.program_id(0)
    count = plan[2 * pools * cap + shift]

    def copy(i):
        return pltpu.make_async_copy(stage.at[i], result.at[plan[shift * cap + i]], sems.at[i])

    @pl.when(slot < count)
    def _():
        total = kept[0]
        for term in arrived:
            total = total + term[0].astype(F32)
        stage[slot] = total.astype(BF16)
        copy(slot).start()

    @pl.when(slot == cap - 1)
    def _():
        for i in range(cap):

            @pl.when(i < count)
            def _(i=i):
                copy(i).wait()


def combine(plan, before, kept, arrived, local_k, shift, pools, cap):
    shape = kept.shape[1:]
    block = pl.BlockSpec((1,) + shape, lambda i, plan: (i, 0, 0, 0))
    operands = ([] if before is None else [before]) + [kept, *arrived]
    return pl.pallas_call(
        functools.partial(combine_kernel, pools, cap, shift, len(arrived)),
        grid_spec=pltpu.PrefetchScalarGridSpec(
            num_scalar_prefetch=1,
            grid=(cap,),
            in_specs=([] if before is None else [ANY]) + [block] * (1 + len(arrived)),
            out_specs=ANY,
            scratch_shapes=[
                pltpu.VMEM((cap,) + shape, BF16), pltpu.SemaphoreType.DMA((cap,)),
            ],
        ),
        out_shape=jax.ShapeDtypeStruct((local_k,) + shape, BF16),
        input_output_aliases={} if before is None else {1: 0},
        compiler_params=pltpu.CompilerParams(vmem_limit_bytes=VMEM_LIMIT),
        cost_estimate=pl.CostEstimate(
            flops=0, bytes_accessed=8 * kept.size, transcendentals=0
        ),
        name="combine",
    )(plan, *operands)


def body(wavefunctions, potentials, pert_order, partners):
    local_k, columns, stacked, bands = wavefunctions.shape
    z_points = stacked // 2
    pools = lax.axis_size("pool")
    groups = lax.axis_size("ga")
    cores = lax.axis_size("pert")
    my_pool = lax.axis_index("pool")
    my_core = lax.axis_index("pert")
    my_group = lax.axis_index("ga")
    cap = max(2, local_k // pools + 1)
    half = columns // cores
    ids = jnp.stack([my_pool, my_core, my_group]).astype(jnp.int32)
    waves = wavefunctions.reshape(local_k * cores, half * stacked, bands)

    plan, sends = make_plan(ids, partners, waves, pools, local_k, cap)
    swap_cores = [(c, cores - 1 - c) for c in range(cores)]
    other_pots = lax.ppermute(potentials, "pert", swap_cores)

    arrivals = {0: (waves, waves)}
    for shift in range(1, pools):
        pairs = [(s, (s + shift) % pools) for s in range(pools)]
        got = lax.ppermute(sends[shift - 1], "pool", pairs)
        arrivals[shift] = (got, lax.ppermute(got, "pert", swap_cores))

    table = dft_table(z_points)
    per_device = potentials.shape[0]
    my_ids = lax.dynamic_slice_in_dim(pert_order, my_core * per_device, per_device)
    stored = jnp.where(my_core == 0, jnp.stack([potentials, other_pots]), jnp.stack([other_pots, potentials]))
    stored = stored.reshape((cores * per_device,) + potentials.shape[1:])
    options = jnp.arange(cores * per_device, dtype=jnp.int32)
    chosen = jnp.sum(
        jnp.where((my_ids[:, None] == options[None, :])[:, :, None, None], stored[None], jnp.zeros((), F32)),
        axis=1,
    )
    chosen = chosen.reshape(per_device, 2, half, 2, z_points)
    chosen = jnp.where(my_core == 0, chosen, chosen[:, ::-1])
    pots = jnp.moveaxis(chosen, 3, 1).reshape(per_device, 2, columns * z_points, 1)
    pots = jnp.broadcast_to(pots, (per_device, 2, columns * z_points, bands))

    scaling = 1.0 / math.sqrt(columns * groups * z_points)
    result = None
    for shift in range(pools):
        kept, gives = couple(
            plan, ids, table, pots, waves, *arrivals[shift], shift, pools, cap, groups, scaling
        )
        terms = [
            lax.ppermute(gives[step - 1], "ga", [(s, (s + step) % groups) for s in range(groups)])
            for step in range(1, groups)
        ]
        result = combine(plan, result, kept, terms, local_k, shift, pools, cap)
    share = bands // groups
    return result.reshape(local_k, per_device, 2, share, bands)


def solution(mesh):
    return jax.shard_map(
        body,
        mesh=mesh,
        in_specs=(P("pool", "ga", None, None), P(("pb", "pert"), "ga", None), P(), P("pb")),
        out_specs=P(("pb", "pool"), "pert", None, "ga", None),
        check_vma=False,
    )
```

```python
import functools
import math

import jax
import jax.numpy as jnp
from jax import lax
from jax.experimental import pallas as pl
from jax.experimental.pallas import tpu as pltpu
from jax.sharding import PartitionSpec as P

BF16 = jnp.bfloat16
F32 = jnp.float32
ANY = pl.BlockSpec(memory_space=pl.ANY)
SMEM = pl.BlockSpec(memory_space=pltpu.SMEM)
VMEM_LIMIT = 60 * 1024 * 1024
LAG_CORE, LAG_MERGE = 2, 3
LIGHT = pl.CostEstimate(flops=1, bytes_accessed=1024, transcendentals=0)


def dft_table(length):
    positions = jnp.arange(length, dtype=jnp.int32)
    product = positions[:, None] * positions[None, :] % length
    angles = product.astype(F32) * (2.0 * math.pi / length)
    cosine = jnp.cos(angles) / math.sqrt(length)
    sine_part = jnp.sin(angles) / math.sqrt(length)
    upper_rows = jnp.concatenate([cosine, -sine_part], axis=1)
    bottom = jnp.concatenate([sine_part, cosine], axis=1)
    return jnp.concatenate([upper_rows, bottom], axis=0).astype(BF16)


def plan_kernel(pools, local_k, cap, ids, partners, plan):
    me = ids[0]
    size = pools * cap
    counts = 3 * size

    def clear(i, carry):
        plan[i] = 0
        return carry

    lax.fori_loop(0, counts + pools, clear, 0, unroll=8)

    def visit(t, tally):
        want = partners[me * local_k + t]
        holder = lax.div(want, local_k)
        shift = lax.rem(me - holder + pools, pools)
        slot = plan[counts + shift]
        plan[shift * cap + slot] = t
        plan[size + shift * cap + slot] = want - holder * local_k
        plan[counts + shift] = slot + 1
        after = []
        for shift in range(1, pools):
            taker = lax.rem(me + shift, pools)
            want = partners[taker * local_k + t]
            slot = tally[shift - 1]
            plan[2 * size + shift * cap + jnp.minimum(slot, cap - 1)] = jnp.where(
                lax.div(want, local_k) == me,
                lax.rem(want, local_k),
                plan[2 * size + shift * cap + jnp.minimum(slot, cap - 1)],
            )
            after.append(slot + (lax.div(want, local_k) == me).astype(jnp.int32))
        return tuple(after)

    lax.fori_loop(0, local_k, visit, (jnp.int32(0),) * (pools - 1), unroll=2)


def make_plan(ids, partners, pools, local_k, cap):
    return pl.pallas_call(
        functools.partial(plan_kernel, pools, local_k, cap),
        out_shape=jax.ShapeDtypeStruct((3 * pools * cap + pools,), jnp.int32),
        in_specs=[SMEM, SMEM],
        out_specs=SMEM,
        name="plan",
    )(ids, partners)


def pick_kernel(plan, ids, source, target):
    target[...] = source[...]


def pick(plan, ids, waves, base, count):
    block = (1,) + waves.shape[1:]
    return pl.pallas_call(
        pick_kernel,
        grid_spec=pltpu.PrefetchScalarGridSpec(
            num_scalar_prefetch=2,
            grid=(count,),
            in_specs=[
                pl.BlockSpec(block, lambda i, plan, ids: (plan[base + i] * 2 + ids[1], 0, 0))
            ],
            out_specs=pl.BlockSpec(block, lambda i, plan, ids: (i, 0, 0)),
        ),
        out_shape=jax.ShapeDtypeStruct((count,) + waves.shape[1:], waves.dtype),
        compiler_params=pltpu.CompilerParams(vmem_limit_bytes=VMEM_LIMIT),
        cost_estimate=LIGHT,
        name="pick",
    )(plan, ids, waves)


def to_real(own, other, table, z_points):
    stacked = 2 * z_points
    bands = own.shape[1]
    parts = [[], [], [], []]
    for c in range(own.shape[0] // stacked):
        rows = slice(c * stacked, (c + 1) * stacked)
        pair = jnp.concatenate([own[rows], other[rows]], axis=1)
        out = jnp.dot(table, pair, preferred_element_type=F32)
        parts[0].append(out[:z_points, :bands])
        parts[1].append(out[z_points:, :bands])
        parts[2].append(out[:z_points, bands:])
        parts[3].append(out[z_points:, bands:])
    return [jnp.concatenate(part, axis=0).astype(BF16) for part in parts]


def couple_kernel(number, first, z_points, scaling, plan, ids, table, pots, own, other, keep, give):
    @pl.when(first + pl.program_id(0) < plan[number])
    def _():
        own_re, own_im, o_re, o_im = to_real(own[0], other[0], table[...], z_points)
        u_re, u_im = own_re.astype(F32), own_im.astype(F32)
        both_o = jnp.concatenate([o_re, o_im], axis=1)
        bands = o_re.shape[1]
        mine = pots.shape[0] // 2
        for j in range(2 * mine):
            p_re, p_im = pots[j, 0], pots[j, 1]
            w_re = (p_re * u_re - p_im * u_im).astype(BF16)
            w_im = (p_re * u_im + p_im * u_re).astype(BF16)
            both = lax.dot_general(
                both_o, jnp.concatenate([w_re, w_im], axis=1),
                (((0,), (0,)), ((), ())), preferred_element_type=F32,
            )
            real = (both[:bands, :bands] + both[bands:, bands:]) * scaling
            imag = (both[:bands, bands:] - both[bands:, :bands]) * scaling
            if j < mine:
                keep[0, 2 * j], keep[0, 2 * j + 1] = real, imag
            else:
                give[0, 2 * (j - mine)] = real.astype(BF16)
                give[0, 2 * (j - mine) + 1] = imag.astype(BF16)


def couple(plan, ids, table, pots, waves, other, chunk, pools, cap, scaling):
    shift, first, count = chunk
    half, bands = waves.shape[1:]
    parts = pots.shape[0]
    base = shift * cap + first
    places = pools * cap + base
    block = (1, half, bands)
    own_block = pl.BlockSpec(block, lambda i, plan, ids: (plan[base + i] * 2 + ids[1], 0, 0))
    if shift == 0:
        other_block = pl.BlockSpec(
            block, lambda i, plan, ids: (plan[places + i] * 2 + ids[1], 0, 0)
        )
    else:
        other_block = pl.BlockSpec(block, lambda i, plan, ids: (i, 0, 0))
    out_block = pl.BlockSpec((1, parts, bands, bands), lambda i, plan, ids: (i, 0, 0, 0))
    return pl.pallas_call(
        functools.partial(
            couple_kernel, 3 * pools * cap + shift, first, table.shape[0] // 2, scaling
        ),
        grid_spec=pltpu.PrefetchScalarGridSpec(
            num_scalar_prefetch=2,
            grid=(count,),
            in_specs=[
                pl.BlockSpec(table.shape, lambda i, plan, ids: (0, 0)),
                pl.BlockSpec(pots.shape, lambda i, plan, ids: (0, 0, 0, 0)),
                own_block, other_block,
            ],
            out_specs=[out_block] * 2,
        ),
        out_shape=[
            jax.ShapeDtypeStruct((count, parts, bands, bands), F32),
            jax.ShapeDtypeStruct((count, parts, bands, bands), BF16),
        ],
        compiler_params=pltpu.CompilerParams(vmem_limit_bytes=VMEM_LIMIT),
        cost_estimate=LIGHT,
        name="couple",
    )(plan, ids, table, pots, waves, other)


def merge_kernel(plan, ids, kept, got, *gives):
    steps = len(gives)
    for i in range(steps):
        gives[i][0] = (kept[0] + got[0].astype(F32)).astype(BF16)


def merge(plan, ids, kept, got, step, groups):
    count, parts, bands, _ = kept.shape
    share = bands // groups
    block = (1, parts, share, bands)
    theirs = pl.BlockSpec(block, lambda i, plan, ids: (i, 0, lax.rem(ids[2] + step, groups), 0))
    return pl.pallas_call(
        merge_kernel,
        grid_spec=pltpu.PrefetchScalarGridSpec(
            num_scalar_prefetch=2,
            grid=(count,),
            in_specs=[theirs, theirs],
            out_specs=[pl.BlockSpec(block, lambda i, plan, ids: (i, 0, 0, 0))],
        ),
        out_shape=[jax.ShapeDtypeStruct((count, parts, share, bands), BF16)],
        compiler_params=pltpu.CompilerParams(vmem_limit_bytes=VMEM_LIMIT),
        cost_estimate=LIGHT,
        name="merge",
    )(plan, ids, kept, got)[0]


def combine_kernel(number, first, length, base, terms, plan, ids, *refs):
    result, stage, sems = refs[-3:]
    summands = refs[-3 - terms : -3]
    slot = pl.program_id(0)
    count = plan[number] - first

    def copy(i):
        return pltpu.make_async_copy(stage.at[i], result.at[plan[base + i]], sems.at[i])

    @pl.when(slot < count)
    def _():
        total = summands[0][0]
        for term in summands[1:]:
            total = total + term[0].astype(F32)
        stage[slot] = total.astype(BF16)
        copy(slot).start()

    @pl.when(slot == length - 1)
    def _():
        for i in range(length):

            @pl.when(i < count)
            def _(i=i):
                copy(i).wait()


def combine(plan, ids, before, kept, got, arrived, local_k, chunk, pools, cap):
    shift, first, length = chunk
    shape = arrived[0].shape[1:]
    block = (1,) + shape
    mine = pl.BlockSpec(block, lambda i, plan, ids: (i, 0, ids[2], 0))
    whole = pl.BlockSpec(block, lambda i, plan, ids: (i, 0, 0, 0))
    terms = [kept, got, *arrived]
    operands = ([] if before is None else [before]) + terms
    return pl.pallas_call(
        functools.partial(
            combine_kernel, 3 * pools * cap + shift, first, length, shift * cap + first,
            len(terms),
        ),
        grid_spec=pltpu.PrefetchScalarGridSpec(
            num_scalar_prefetch=2,
            grid=(length,),
            in_specs=([] if before is None else [ANY]) + [mine] * 2 + [whole] * len(arrived),
            out_specs=ANY,
            scratch_shapes=[
                pltpu.VMEM((length,) + shape, BF16), pltpu.SemaphoreType.DMA((length,)),
            ],
        ),
        out_shape=jax.ShapeDtypeStruct((local_k,) + shape, BF16),
        input_output_aliases={} if before is None else {2: 0},
        compiler_params=pltpu.CompilerParams(vmem_limit_bytes=VMEM_LIMIT),
        cost_estimate=LIGHT,
        name="combine",
    )(plan, ids, *operands)


def body(wavefunctions, potentials, pert_order, partners):
    local_k, columns, stacked, bands = wavefunctions.shape
    z_points = stacked // 2
    pools = lax.axis_size("pool")
    groups = lax.axis_size("ga")
    cores = lax.axis_size("pert")
    my_pool = lax.axis_index("pool")
    my_core = lax.axis_index("pert")
    my_group = lax.axis_index("ga")
    cap = max(2, local_k // pools + 1)
    half = columns // cores
    ids = jnp.stack([my_pool, my_core, my_group]).astype(jnp.int32)
    waves = wavefunctions.reshape(local_k * cores, half * stacked, bands)

    plan = make_plan(ids, partners, pools, local_k, cap)
    swap_cores = [(c, cores - 1 - c) for c in range(cores)]
    per_device = potentials.shape[0]
    chunks = []
    for shift in sorted(range(1, pools), key=lambda d: min(d, pools - d)):
        cuts = [0, cap] if 2 * shift != pools else [0, (cap + 1) // 2, cap]
        chunks += [(shift, lo, hi - lo) for lo, hi in zip(cuts, cuts[1:])]
    landed, gives = [], []
    for shift, first, count in chunks:
        gives.append(pick(plan, ids, waves, 2 * pools * cap + shift * cap + first, count))
    here, potentials, *gives = lax.optimization_barrier((waves, potentials, *gives))
    for (shift, first, count), give in zip(chunks, gives):
        pairs = [(s, (s + shift) % pools) for s in range(pools)]
        landed.append(lax.ppermute(give, "pool", pairs))

    table = dft_table(z_points)
    by_half = potentials.reshape(per_device, cores, half, stacked)
    mine_now = lax.dynamic_index_in_dim(by_half, my_core, 1, keepdims=False)
    theirs_now = lax.dynamic_index_in_dim(by_half, 1 - my_core, 1, keepdims=False)
    other_pots = lax.ppermute(theirs_now, "pert", swap_cores)

    ordered = jnp.roll(pert_order.reshape(cores, per_device), -my_core, axis=0).reshape(-1)
    stored = jnp.where(
        my_core == 0, jnp.stack([mine_now, other_pots]), jnp.stack([other_pots, mine_now])
    ).reshape((cores * per_device,) + mine_now.shape[1:])
    options = jnp.arange(cores * per_device, dtype=jnp.int32)
    chosen = jnp.sum(
        jnp.where(
            (ordered[:, None] == options[None, :])[:, :, None, None], stored[None],
            jnp.zeros((), F32),
        ),
        axis=1,
    ).reshape(cores * per_device, half, 2, z_points)
    pots = jnp.moveaxis(chosen, 2, 1).reshape(cores * per_device, 2, half * z_points, 1)
    pots = jnp.broadcast_to(pots, pots.shape[:3] + (bands,))

    scaling = 1.0 / math.sqrt(columns * groups * z_points)

    result = None
    chunks = [(0, 0, cap)] + chunks
    landed = [here] + landed
    kept, got, terms = [], [], []

    def send_on(i):
        swapped = got[i]
        terms.append([
            lax.ppermute(
                merge(plan, ids, kept[i], swapped, step, groups), "ga",
                [(s, (s + step) % groups) for s in range(groups)],
            )
            for step in range(1, groups)
        ])

    def finish(i, result):
        return combine(
            plan, ids, result, kept[i], got[i], terms[i], local_k, chunks[i], pools, cap
        )

    last = len(chunks) - 1
    for i, chunk in enumerate(chunks):
        arrived = landed[i]
        if i >= 1:
            arrived, kept[i - 1] = lax.optimization_barrier((arrived, kept[i - 1]))
        if i >= LAG_CORE:
            arrived, got[i - LAG_CORE] = lax.optimization_barrier((arrived, got[i - LAG_CORE]))
            send_on(i - LAG_CORE)
        if i >= LAG_MERGE and i - LAG_MERGE < len(terms):
            arrived, terms[i - LAG_MERGE] = lax.optimization_barrier((arrived, terms[i - LAG_MERGE]))
        keep, give = couple(plan, ids, table, pots, waves, arrived, chunk, pools, cap, scaling)
        kept.append(keep)
        got.append(lax.ppermute(give, "pert", swap_cores))
    for i in range(len(terms), len(chunks)):
        send_on(i)
    for i in range(len(chunks)):
        result = finish(i, result)
    share = bands // groups
    return result.reshape(local_k, per_device, 2, share, bands)


def solution(mesh):
    return jax.shard_map(
        body,
        mesh=mesh,
        in_specs=(P("pool", "ga", None, None), P(("pb", "pert"), "ga", None), P(), P("pb")),
        out_specs=P(("pb", "pool"), "pert", None, "ga", None),
        check_vma=False,
    )
```

```python
import functools
import math

import jax
import jax.numpy as jnp
from jax import lax
from jax.experimental import pallas as pl
from jax.experimental.pallas import tpu as pltpu
from jax.sharding import PartitionSpec as P

BF16 = jnp.bfloat16
F32 = jnp.float32
ANY = pl.BlockSpec(memory_space=pl.ANY)
SMEM = pl.BlockSpec(memory_space=pltpu.SMEM)
VMEM_LIMIT = 60 * 1024 * 1024
LIGHT = pl.CostEstimate(flops=1, bytes_accessed=1024, transcendentals=0)
PARAMS = pltpu.CompilerParams(vmem_limit_bytes=VMEM_LIMIT)


def dft_table(length):
    positions = jnp.arange(length, dtype=jnp.int32)
    product = positions[:, None] * positions[None, :] % length
    angles = product.astype(F32) * (2.0 * math.pi / length)
    cosine = jnp.cos(angles) / math.sqrt(length)
    sine_part = jnp.sin(angles) / math.sqrt(length)
    upper_rows = jnp.concatenate([cosine, -sine_part], axis=1)
    bottom = jnp.concatenate([sine_part, cosine], axis=1)
    return jnp.concatenate([upper_rows, bottom], axis=0).astype(BF16)


def plan_kernel(pools, local_k, cap, ids, partners, plan):
    me = ids[0]
    size = pools * cap
    counts = 3 * size

    def clear(i, carry):
        plan[i] = 0
        return carry

    lax.fori_loop(0, counts + pools, clear, 0, unroll=8)

    def visit(t, tally):
        want = partners[me * local_k + t]
        holder = lax.div(want, local_k)
        shift = lax.rem(me - holder + pools, pools)
        slot = plan[counts + shift]
        plan[shift * cap + slot] = t
        plan[size + shift * cap + slot] = want - holder * local_k
        plan[counts + shift] = slot + 1
        after = []
        for shift in range(1, pools):
            taker = lax.rem(me + shift, pools)
            want = partners[taker * local_k + t]
            slot = tally[shift - 1]
            mine = lax.div(want, local_k) == me
            entry = 2 * size + shift * cap + jnp.minimum(slot, cap - 1)
            plan[entry] = jnp.where(mine, lax.rem(want, local_k), plan[entry])
            after.append(slot + mine.astype(jnp.int32))
        return tuple(after)

    lax.fori_loop(0, local_k, visit, (jnp.int32(0),) * (pools - 1), unroll=2)


def make_plan(ids, partners, pools, local_k, cap):
    return pl.pallas_call(
        functools.partial(plan_kernel, pools, local_k, cap),
        out_shape=jax.ShapeDtypeStruct((3 * pools * cap + pools,), jnp.int32),
        in_specs=[SMEM, SMEM],
        out_specs=SMEM,
        cost_estimate=LIGHT,
        name="plan",
    )(ids, partners)


def pick_kernel(base, cap, count, pools, plan, ids, waves, give, sems):
    copies = []
    for shift in range(1, pools):
        taker = lax.rem(ids[0] + shift, pools)
        for i in range(count):
            place = plan[base + shift * cap + i] * 2 + ids[1]
            copies.append(
                pltpu.make_async_copy(waves.at[place], give.at[taker, i], sems.at[shift - 1, i])
            )
    for copy in copies:
        copy.start()
    for copy in copies:
        copy.wait()


def pick(plan, ids, waves, pools, cap, first, count):
    return pl.pallas_call(
        functools.partial(pick_kernel, 2 * pools * cap + first, cap, count, pools),
        out_shape=jax.ShapeDtypeStruct((pools, count) + waves.shape[1:], waves.dtype),
        in_specs=[SMEM, SMEM, ANY],
        out_specs=pl.BlockSpec(memory_space=pltpu.VMEM),
        scratch_shapes=[pltpu.SemaphoreType.DMA((pools - 1, count))],
        compiler_params=PARAMS,
        cost_estimate=LIGHT,
        name="pick",
    )(plan, ids, waves)


def to_real(own, other, table, z_points):
    stacked = 2 * z_points
    bands = own.shape[1]
    parts = [[], [], [], []]
    for c in range(own.shape[0] // stacked):
        rows = slice(c * stacked, (c + 1) * stacked)
        pair = jnp.concatenate([own[rows], other[rows]], axis=1)
        out = jnp.dot(table, pair, preferred_element_type=F32)
        parts[0].append(out[:z_points, :bands])
        parts[1].append(out[z_points:, :bands])
        parts[2].append(out[:z_points, bands:])
        parts[3].append(out[z_points:, bands:])
    return [jnp.concatenate(part, axis=0).astype(BF16) for part in parts]


def couple_kernel(shape, plan, ids, table, pots, own, *rest):
    counts, cap, shift, first, count, groups, z_points = shape
    other, keep, give = rest
    i = pl.program_id(0)
    source = i // count

    @pl.when(first + i - source * count < plan[counts + shift + source])
    def _():
        own_re, own_im, o_re, o_im = to_real(
            own[0], other[...].reshape(own.shape[1:]), table[...], z_points
        )
        u_re, u_im = own_re.astype(F32), own_im.astype(F32)
        both_o = jnp.concatenate([o_re, o_im], axis=1).T
        bands = o_re.shape[1]
        share = bands // groups
        mine = pots.shape[0] // 2
        starts = [
            pl.multiple_of(lax.rem(g - ids[2] + groups, groups) * share, share)
            for g in range(groups)
        ]
        for j in range(2 * mine):
            p_re, p_im = pots[j, 0], pots[j, 1]
            w_re = (p_re * u_re - p_im * u_im).astype(BF16)
            w_im = (p_re * u_im + p_im * u_re).astype(BF16)
            both = jnp.dot(
                both_o, jnp.concatenate([w_re, w_im], axis=1), preferred_element_type=F32
            )
            real = both[:bands, :bands] + both[bands:, bands:]
            imag = both[:bands, bands:] - both[bands:, :bands]
            for part, value in ((0, real), (1, imag)):
                for g in range(groups):
                    rows = value[g * share : (g + 1) * share]
                    if j < mine:
                        keep[0, 2 * j + part, pl.ds(starts[g], share), :] = rows
                    else:
                        place = 2 * (j - mine) + part
                        give[0, place, pl.ds(starts[g], share), :] = rows.astype(BF16)


def couple(plan, ids, table, pots, waves, other, chunk, pools, cap, groups):
    shift, first, count = chunk
    half, bands = waves.shape[1:]
    parts = pots.shape[0]
    sources = 1 if shift == 0 else pools - 1
    block = (1, half, bands)

    def entry(i):
        return (shift + i // count) * cap + first + i % count

    own_block = pl.BlockSpec(block, lambda i, plan, ids: (plan[entry(i)] * 2 + ids[1], 0, 0))
    if shift == 0:
        other_block = pl.BlockSpec(
            block, lambda i, plan, ids: (plan[pools * cap + entry(i)] * 2 + ids[1], 0, 0)
        )
    else:
        other_block = pl.BlockSpec(
            (1,) + block,
            lambda i, plan, ids: (
                lax.rem(ids[0] - shift - i // count + pools, pools), i % count, 0, 0
            ),
        )
    out_block = pl.BlockSpec((1, parts, bands, bands), lambda i, plan, ids: (i, 0, 0, 0))
    shape = (3 * pools * cap, cap, shift, first, count, groups, table.shape[0] // 2)
    total = sources * count
    return pl.pallas_call(
        functools.partial(couple_kernel, shape),
        grid_spec=pltpu.PrefetchScalarGridSpec(
            num_scalar_prefetch=2,
            grid=(total,),
            in_specs=[
                pl.BlockSpec(table.shape, lambda i, plan, ids: (0, 0)),
                pl.BlockSpec(pots.shape, lambda i, plan, ids: (0, 0, 0, 0)),
                own_block, other_block,
            ],
            out_specs=[out_block] * 2,
        ),
        out_shape=[
            jax.ShapeDtypeStruct((total, parts, bands, bands), F32),
            jax.ShapeDtypeStruct((total, parts, bands, bands), BF16),
        ],
        compiler_params=PARAMS,
        cost_estimate=LIGHT,
        name="couple",
    )(plan, ids, table, pots, waves, other)


def combine_kernel(shape, scaling, plan, *refs):
    counts, cap, shift, first, count, total, terms = shape
    result, stage, sems = refs[-3:]
    summands = refs[-3 - terms : -3]

    def each(action):
        for i in range(total):
            source, slot = shift + i // count, first + i % count

            @pl.when(slot < plan[counts + source])
            def _(i=i, source=source, slot=slot):
                action(i, pltpu.make_async_copy(
                    stage.at[i], result.at[plan[source * cap + slot]], sems.at[i]
                ))

    def add(i, copy):
        value = summands[0][i]
        for term in summands[1:]:
            value = value + term[i].astype(F32)
        stage[i] = (value * scaling).astype(BF16)
        copy.start()

    each(add)
    each(lambda i, copy: copy.wait())


def combine(plan, before, kept, got, arrived, local_k, chunk, pools, cap, scaling):
    shift, first, count = chunk
    total = kept.shape[0]
    shape = arrived[0].shape
    block = pl.BlockSpec(shape, lambda i, plan: (0, 0, 0, 0))
    terms = [kept, got, *arrived]
    operands = ([] if before is None else [before]) + terms
    return pl.pallas_call(
        functools.partial(
            combine_kernel, (3 * pools * cap, cap, shift, first, count, total, len(terms)), scaling
        ),
        grid_spec=pltpu.PrefetchScalarGridSpec(
            num_scalar_prefetch=1,
            grid=(1,),
            in_specs=([] if before is None else [ANY]) + [block] * len(terms),
            out_specs=ANY,
            scratch_shapes=[pltpu.VMEM(shape, BF16), pltpu.SemaphoreType.DMA((total,))],
        ),
        out_shape=jax.ShapeDtypeStruct((local_k,) + shape[1:], BF16),
        input_output_aliases={} if before is None else {1: 0},
        compiler_params=PARAMS,
        cost_estimate=LIGHT,
        name="combine",
    )(plan, *operands)


def after(value, *others):
    return lax.optimization_barrier((value, *others))[0]


def body(wavefunctions, potentials, pert_order, partners):
    local_k, columns, stacked, bands = wavefunctions.shape
    z_points = stacked // 2
    pools = lax.axis_size("pool")
    groups = lax.axis_size("ga")
    cores = lax.axis_size("pert")
    my_pool = lax.axis_index("pool")
    my_core = lax.axis_index("pert")
    my_group = lax.axis_index("ga")
    cap = max(2, local_k // pools + 1)
    half = columns // cores
    share = bands // groups
    ids = jnp.stack([my_pool, my_core, my_group]).astype(jnp.int32)
    waves = wavefunctions.reshape(local_k * cores, half * stacked, bands)
    swap_cores = [(c, cores - 1 - c) for c in range(cores)]

    plan = make_plan(ids, partners, pools, local_k, cap)
    step = -(-cap // 3)
    phases = [(first, min(step, cap - first)) for first in range(0, cap, step)]
    gives = [pick(plan, ids, waves, pools, cap, first, count) for first, count in phases]
    potentials = after(potentials, gives[0])

    per_device = potentials.shape[0]
    by_half = potentials.reshape(per_device, cores, half, stacked)
    mine_now = lax.dynamic_index_in_dim(by_half, my_core, 1, keepdims=False)
    theirs_now = lax.dynamic_index_in_dim(by_half, 1 - my_core, 1, keepdims=False)
    other_pots = lax.ppermute(theirs_now, "pert", swap_cores)
    ordered = jnp.roll(pert_order.reshape(cores, per_device), -my_core, axis=0).reshape(-1)
    stored = jnp.where(
        my_core == 0, jnp.stack([mine_now, other_pots]), jnp.stack([other_pots, mine_now])
    ).reshape((cores * per_device,) + mine_now.shape[1:])
    options = jnp.arange(cores * per_device, dtype=jnp.int32)
    chosen = jnp.sum(
        jnp.where(
            (ordered[:, None] == options[None, :])[:, :, None, None], stored[None],
            jnp.zeros((), F32),
        ),
        axis=1,
    ).reshape(cores * per_device, half, 2, z_points)
    pots = jnp.moveaxis(chosen, 2, 1).reshape(cores * per_device, 2, half * z_points, 1)
    pots = jnp.broadcast_to(pots, pots.shape[:3] + (bands,))
    table = dft_table(z_points)
    scaling = 1.0 / math.sqrt(columns * groups * z_points)

    landed = []
    for phase, give in enumerate(gives):
        if phase >= WINDOW:
            give = after(give, landed[phase - WINDOW])
        landed.append(lax.all_to_all(give, "pool", 0, 0, tiled=True))

    chunks = [((0, 0, cap), waves)]
    chunks += [((1, first, count), row) for (first, count), row in zip(phases, landed)]
    kept, got, terms = [], [], []
    result = None

    def exchange(i):
        sent = []
        for step in range(1, groups):
            rows = slice(step * share, (step + 1) * share)
            total = (kept[i][:, :, rows] + got[i][:, :, rows].astype(F32)).astype(BF16)
            pairs = [(g, (g + step) % groups) for g in range(groups)]
            sent.append(lax.ppermute(total, "ga", pairs))
        terms.append(sent)

    def finish(i, result):
        return combine(
            plan, result, kept[i], got[i], terms[i], local_k, chunks[i][0], pools, cap, scaling
        )

    for i, (chunk, other) in enumerate(chunks):
        if i >= 1:
            other = after(other, kept[i - 1])
        if i >= LAG_CORE:
            exchange(i - LAG_CORE)
            other = after(other, got[i - LAG_CORE])
        if i >= LAG_GROUP:
            result = finish(i - LAG_GROUP, result)
            other = after(other, result)
        keep, give = couple(plan, ids, table, pots, waves, other, chunk, pools, cap, groups)
        kept.append(keep)
        got.append(lax.ppermute(give, "pert", swap_cores))
    for i in range(len(terms), len(chunks)):
        exchange(i)
    for i in range(max(0, len(chunks) - LAG_GROUP), len(chunks)):
        result = finish(i, result)
    return result.reshape(local_k, per_device, 2, share, bands)


WINDOW = 1
LAG_CORE, LAG_GROUP = 1, 2


def solution(mesh):
    return jax.shard_map(
        body,
        mesh=mesh,
        in_specs=(P("pool", "ga", None, None), P(("pb", "pert"), "ga", None), P(), P("pb")),
        out_specs=P(("pb", "pool"), "pert", None, "ga", None),
        check_vma=False,
    )
```

```python
import functools
import math

import jax
import jax.numpy as jnp
from jax import lax
from jax.experimental import pallas as pl
from jax.experimental.pallas import tpu as pltpu
from jax.sharding import PartitionSpec as P

BF16 = jnp.bfloat16
F32 = jnp.float32
ANY = pl.BlockSpec(memory_space=pl.ANY)
SMEM = pl.BlockSpec(memory_space=pltpu.SMEM)
VMEM_LIMIT = 60 * 1024 * 1024
LIGHT = pl.CostEstimate(flops=1, bytes_accessed=1024, transcendentals=0)
PARAMS = pltpu.CompilerParams(vmem_limit_bytes=VMEM_LIMIT)


def dft_table(length):
    positions = jnp.arange(length, dtype=jnp.int32)
    product = positions[:, None] * positions[None, :] % length
    angles = product.astype(F32) * (2.0 * math.pi / length)
    cosine = jnp.cos(angles) / math.sqrt(length)
    sine_part = jnp.sin(angles) / math.sqrt(length)
    upper_rows = jnp.concatenate([cosine, -sine_part], axis=1)
    bottom = jnp.concatenate([sine_part, cosine], axis=1)
    return jnp.concatenate([upper_rows, bottom], axis=0).astype(BF16)


def plan_kernel(pools, local_k, cap, ids, partners, plan):
    me = ids[0]
    size = pools * cap
    counts = 3 * size

    def clear(i, carry):
        plan[i] = 0
        return carry

    lax.fori_loop(0, counts + pools, clear, 0, unroll=8)

    def visit(t, tally):
        want = partners[me * local_k + t]
        holder = lax.div(want, local_k)
        shift = lax.rem(me - holder + pools, pools)
        slot = plan[counts + shift]
        plan[shift * cap + slot] = t
        plan[size + shift * cap + slot] = want - holder * local_k
        plan[counts + shift] = slot + 1
        after = []
        for shift in range(1, pools):
            taker = lax.rem(me + shift, pools)
            want = partners[taker * local_k + t]
            slot = tally[shift - 1]
            mine = lax.div(want, local_k) == me
            entry = 2 * size + shift * cap + jnp.minimum(slot, cap - 1)
            plan[entry] = jnp.where(mine, lax.rem(want, local_k), plan[entry])
            after.append(slot + mine.astype(jnp.int32))
        return tuple(after)

    lax.fori_loop(0, local_k, visit, (jnp.int32(0),) * (pools - 1), unroll=2)


def make_plan(ids, partners, pools, local_k, cap):
    return pl.pallas_call(
        functools.partial(plan_kernel, pools, local_k, cap),
        out_shape=jax.ShapeDtypeStruct((3 * pools * cap + pools,), jnp.int32),
        in_specs=[SMEM, SMEM],
        out_specs=SMEM,
        cost_estimate=LIGHT,
        name="plan",
    )(ids, partners)


def pick_kernel(base, plan, ids, waves, give, sems):
    copies = [
        pltpu.make_async_copy(waves.at[plan[base + i] * 2 + ids[1]], give.at[i], sems.at[i])
        for i in range(give.shape[0])
    ]
    for copy in copies:
        copy.start()
    for copy in copies:
        copy.wait()


def pick(plan, ids, waves, pools, cap, chunk):
    shift, first, count = chunk
    return pl.pallas_call(
        functools.partial(pick_kernel, (2 * pools + shift) * cap + first),
        out_shape=jax.ShapeDtypeStruct((count,) + waves.shape[1:], waves.dtype),
        in_specs=[SMEM, SMEM, ANY],
        out_specs=pl.BlockSpec(memory_space=pltpu.VMEM),
        scratch_shapes=[pltpu.SemaphoreType.DMA((count,))],
        compiler_params=PARAMS,
        cost_estimate=LIGHT,
        name="pick",
    )(plan, ids, waves)


def to_real(own, other, table, z_points):
    stacked = 2 * z_points
    bands = own.shape[1]
    parts = [[], [], [], []]
    for c in range(own.shape[0] // stacked):
        rows = slice(c * stacked, (c + 1) * stacked)
        pair = jnp.concatenate([own[rows], other[rows]], axis=1)
        out = jnp.dot(table, pair, preferred_element_type=F32)
        parts[0].append(out[:z_points, :bands])
        parts[1].append(out[z_points:, :bands])
        parts[2].append(out[:z_points, bands:])
        parts[3].append(out[z_points:, bands:])
    return [jnp.concatenate(part, axis=0).astype(BF16) for part in parts]


def couple_kernel(shape, plan, ids, table, pots, own, other, keep, give):
    number, first, groups, z_points = shape

    @pl.when(first + pl.program_id(0) < plan[number])
    def _():
        own_re, own_im, o_re, o_im = to_real(own[0], other[0], table[...], z_points)
        u_re, u_im = own_re.astype(F32), own_im.astype(F32)
        both_o = jnp.concatenate([o_re, o_im], axis=1).T
        bands = o_re.shape[1]
        share = bands // groups
        mine = pots.shape[0] // 2
        starts = [
            pl.multiple_of(lax.rem(g - ids[2] + groups, groups) * share, share)
            for g in range(groups)
        ]
        for j in range(2 * mine):
            p_re, p_im = pots[j, 0], pots[j, 1]
            w_re = (p_re * u_re - p_im * u_im).astype(BF16)
            w_im = (p_re * u_im + p_im * u_re).astype(BF16)
            both = jnp.dot(
                both_o, jnp.concatenate([w_re, w_im], axis=1), preferred_element_type=F32
            )
            real = both[:bands, :bands] + both[bands:, bands:]
            imag = both[:bands, bands:] - both[bands:, :bands]
            for part, value in ((0, real), (1, imag)):
                for g in range(groups):
                    rows = value[g * share : (g + 1) * share]
                    if j < mine:
                        keep[0, 2 * j + part, pl.ds(starts[g], share), :] = rows
                    else:
                        place = 2 * (j - mine) + part
                        give[0, place, pl.ds(starts[g], share), :] = rows.astype(BF16)


def couple(plan, ids, table, pots, waves, other, chunk, pools, cap, groups):
    shift, first, count = chunk
    half, bands = waves.shape[1:]
    parts = pots.shape[0]
    base = shift * cap + first
    block = (1, half, bands)
    own_block = pl.BlockSpec(block, lambda i, plan, ids: (plan[base + i] * 2 + ids[1], 0, 0))
    if shift == 0:
        other_block = pl.BlockSpec(
            block, lambda i, plan, ids: (plan[pools * cap + base + i] * 2 + ids[1], 0, 0)
        )
    else:
        other_block = pl.BlockSpec(block, lambda i, plan, ids: (i, 0, 0))
    out_block = pl.BlockSpec((1, parts, bands, bands), lambda i, plan, ids: (i, 0, 0, 0))
    shape = (3 * pools * cap + shift, first, groups, table.shape[0] // 2)
    return pl.pallas_call(
        functools.partial(couple_kernel, shape),
        grid_spec=pltpu.PrefetchScalarGridSpec(
            num_scalar_prefetch=2,
            grid=(count,),
            in_specs=[
                pl.BlockSpec(table.shape, lambda i, plan, ids: (0, 0)),
                pl.BlockSpec(pots.shape, lambda i, plan, ids: (0, 0, 0, 0)),
                own_block, other_block,
            ],
            out_specs=[out_block] * 2,
        ),
        out_shape=[
            jax.ShapeDtypeStruct((count, parts, bands, bands), F32),
            jax.ShapeDtypeStruct((count, parts, bands, bands), BF16),
        ],
        compiler_params=PARAMS,
        cost_estimate=LIGHT,
        name="couple",
    )(plan, ids, table, pots, waves, other)


def combine_kernel(shape, scaling, plan, *refs):
    number, base, first, total, pieces, others = shape
    result, stage, sems = refs[-3:]
    summands = refs[-3 - 1 - pieces * (1 + others) : -3]
    size = summands[1].shape[0]

    def each(action):
        for i in range(total):

            @pl.when(first + i < plan[number])
            def _(i=i):
                action(i, pltpu.make_async_copy(
                    stage.at[i], result.at[plan[base + i]], sems.at[i]
                ))

    def add(i, copy):
        value = summands[0][i]
        for group in range(1 + others):
            value = value + summands[1 + group * pieces + i // size][i % size].astype(F32)
        stage[i] = (value * scaling).astype(BF16)
        copy.start()

    each(add)
    each(lambda i, copy: copy.wait())


def combine(plan, before, kept, got, arrived, local_k, chunk, pools, cap, scaling):
    shift, first, count = chunk
    _, parts, _, bands = kept.shape
    share = arrived[0].shape[2]
    terms = [kept, *got, *arrived]
    blocks = [
        pl.BlockSpec((term.shape[0], parts, share, bands), lambda i, plan: (0, 0, 0, 0))
        for term in terms
    ]
    operands = ([] if before is None else [before]) + terms
    shape = (
        3 * pools * cap + shift, shift * cap + first, first, count, len(got),
        len(arrived) // len(got),
    )
    return pl.pallas_call(
        functools.partial(combine_kernel, shape, scaling),
        grid_spec=pltpu.PrefetchScalarGridSpec(
            num_scalar_prefetch=1,
            grid=(1,),
            in_specs=([] if before is None else [ANY]) + blocks,
            out_specs=ANY,
            scratch_shapes=[
                pltpu.VMEM((count, parts, share, bands), BF16),
                pltpu.SemaphoreType.DMA((count,)),
            ],
        ),
        out_shape=jax.ShapeDtypeStruct((local_k, parts, share, bands), BF16),
        input_output_aliases={} if before is None else {1: 0},
        compiler_params=PARAMS,
        cost_estimate=LIGHT,
        name="combine",
    )(plan, *operands)


def after(value, *others):
    return lax.optimization_barrier((value, *others))[0]


def transfers(pools, cap):
    moves, waits = [], []
    for s in range(1, (pools + 1) // 2):
        for shift in (s, pools - s):
            moves.append((shift, 0, cap))
            waits.append(len(moves) - 3 if s > 1 else None)
    if pools % 2 == 0:
        large = (3 * cap + 2) // 5
        for first, count in ((0, large), (large, cap - large)):
            moves.append((pools // 2, first, count))
            waits.append(len(moves) - 2 if len(moves) > 1 else None)
    return moves, waits


def body(wavefunctions, potentials, pert_order, partners):
    local_k, columns, stacked, bands = wavefunctions.shape
    z_points = stacked // 2
    pools = lax.axis_size("pool")
    groups = lax.axis_size("ga")
    cores = lax.axis_size("pert")
    my_pool = lax.axis_index("pool")
    my_core = lax.axis_index("pert")
    my_group = lax.axis_index("ga")
    cap = max(2, local_k // pools + 1)
    half = columns // cores
    share = bands // groups
    ids = jnp.stack([my_pool, my_core, my_group]).astype(jnp.int32)
    waves = wavefunctions.reshape(local_k * cores, half * stacked, bands)
    swap_cores = [(c, cores - 1 - c) for c in range(cores)]

    plan = make_plan(ids, partners, pools, local_k, cap)
    moves, waits = transfers(pools, cap)
    gives = [pick(plan, ids, waves, pools, cap, move) for move in moves]
    potentials = after(potentials, gives[0])

    per_device = potentials.shape[0]
    by_half = potentials.reshape(per_device, cores, half, stacked)
    mine_now = lax.dynamic_index_in_dim(by_half, my_core, 1, keepdims=False)
    theirs_now = lax.dynamic_index_in_dim(by_half, 1 - my_core, 1, keepdims=False)
    other_pots = lax.ppermute(theirs_now, "pert", swap_cores)
    ordered = jnp.roll(pert_order.reshape(cores, per_device), -my_core, axis=0).reshape(-1)
    stored = jnp.where(
        my_core == 0, jnp.stack([mine_now, other_pots]), jnp.stack([other_pots, mine_now])
    ).reshape((cores * per_device,) + mine_now.shape[1:])
    options = jnp.arange(cores * per_device, dtype=jnp.int32)
    chosen = jnp.sum(
        jnp.where(
            (ordered[:, None] == options[None, :])[:, :, None, None], stored[None],
            jnp.zeros((), F32),
        ),
        axis=1,
    ).reshape(cores * per_device, half, 2, z_points)
    pots = jnp.moveaxis(chosen, 2, 1).reshape(cores * per_device, 2, half * z_points, 1)
    pots = jnp.broadcast_to(pots, pots.shape[:3] + (bands,))
    table = dft_table(z_points)
    scaling = 1.0 / math.sqrt(columns * groups * z_points)

    landed = []
    for move, wait, give in zip(moves, waits, gives):
        if wait is not None:
            give = after(give, landed[wait])
        pairs = [(p, (p + move[0]) % pools) for p in range(pools)]
        landed.append(lax.ppermute(give, "pool", pairs))

    chunks = [((0, 0, cap), waves), *zip(moves, landed)]
    kept, got, terms = [], [], []
    result = None

    def swap(give):
        return [
            lax.ppermute(give[first : first + PIECE], "pert", swap_cores)
            for first in range(0, give.shape[0], PIECE)
        ]

    def exchange(i):
        sent = []
        for step in range(1, groups):
            rows = slice(step * share, (step + 1) * share)
            pairs = [(g, (g + step) % groups) for g in range(groups)]
            for at, piece in enumerate(got[i]):
                mine = kept[i][at * PIECE : at * PIECE + piece.shape[0]]
                total = (mine[:, :, rows] + piece[:, :, rows].astype(F32)).astype(BF16)
                sent.append(lax.ppermute(total, "ga", pairs))
        terms.append(sent)

    def finish(i, result):
        return combine(
            plan, result, kept[i], got[i], terms[i], local_k, chunks[i][0], pools, cap, scaling
        )

    for i, (chunk, other) in enumerate(chunks):
        if i >= 1:
            other = after(other, kept[i - 1])
        if i >= LAG_CORE:
            exchange(i - LAG_CORE)
            other = after(other, *got[i - LAG_CORE])
        if i >= LAG_GROUP:
            result = finish(i - LAG_GROUP, result)
            other = after(other, result)
        keep, give = couple(plan, ids, table, pots, waves, other, chunk, pools, cap, groups)
        kept.append(keep)
        got.append(swap(give))
    for i in range(len(terms), len(chunks)):
        exchange(i)
    for i in range(max(0, len(chunks) - LAG_GROUP), len(chunks)):
        result = finish(i, result)
    return result.reshape(local_k, per_device, 2, share, bands)


LAG_CORE, LAG_GROUP = 1, 2
PIECE = 3


def solution(mesh):
    return jax.shard_map(
        body,
        mesh=mesh,
        in_specs=(P("pool", "ga", None, None), P(("pb", "pert"), "ga", None), P(), P("pb")),
        out_specs=P(("pb", "pool"), "pert", None, "ga", None),
        check_vma=False,
    )
```

```python
import functools
import math

import jax
import jax.numpy as jnp
from jax import lax
from jax.experimental import pallas as pl
from jax.experimental.pallas import tpu as pltpu
from jax.sharding import PartitionSpec as P

BF16 = jnp.bfloat16
F32 = jnp.float32
ANY = pl.BlockSpec(memory_space=pl.ANY)
SMEM = pl.BlockSpec(memory_space=pltpu.SMEM)
VMEM_LIMIT = 60 * 1024 * 1024
LIGHT = pl.CostEstimate(flops=1, bytes_accessed=1024, transcendentals=0)
PARAMS = pltpu.CompilerParams(vmem_limit_bytes=VMEM_LIMIT)


def dft_table(length):
    positions = jnp.arange(length, dtype=jnp.int32)
    product = positions[:, None] * positions[None, :] % length
    angles = product.astype(F32) * (2.0 * math.pi / length)
    cosine = jnp.cos(angles) / math.sqrt(length)
    sine_part = jnp.sin(angles) / math.sqrt(length)
    upper_rows = jnp.concatenate([cosine, -sine_part], axis=1)
    bottom = jnp.concatenate([sine_part, cosine], axis=1)
    return jnp.concatenate([upper_rows, bottom], axis=0).astype(BF16)


def plan_kernel(pools, local_k, cap, ids, partners, plan):
    me = ids[0]
    size = pools * cap
    counts = 3 * size

    def clear(i, carry):
        plan[i] = 0
        return carry

    lax.fori_loop(0, counts + pools, clear, 0, unroll=8)

    def visit(t, tally):
        want = partners[me * local_k + t]
        holder = lax.div(want, local_k)
        shift = lax.rem(me - holder + pools, pools)
        slot = plan[counts + shift]
        plan[shift * cap + slot] = t
        plan[size + shift * cap + slot] = want - holder * local_k
        plan[counts + shift] = slot + 1
        after = []
        for shift in range(1, pools):
            taker = lax.rem(me + shift, pools)
            want = partners[taker * local_k + t]
            slot = tally[shift - 1]
            mine = lax.div(want, local_k) == me
            entry = 2 * size + shift * cap + jnp.minimum(slot, cap - 1)
            plan[entry] = jnp.where(mine, lax.rem(want, local_k), plan[entry])
            after.append(slot + mine.astype(jnp.int32))
        return tuple(after)

    lax.fori_loop(0, local_k, visit, (jnp.int32(0),) * (pools - 1), unroll=2)


def make_plan(ids, partners, pools, local_k, cap):
    return pl.pallas_call(
        functools.partial(plan_kernel, pools, local_k, cap),
        out_shape=jax.ShapeDtypeStruct((3 * pools * cap + pools,), jnp.int32),
        in_specs=[SMEM, SMEM],
        out_specs=SMEM,
        cost_estimate=LIGHT,
        name="plan",
    )(ids, partners)


def pick_kernel(base, plan, ids, waves, give, sems):
    copies = [
        pltpu.make_async_copy(waves.at[plan[base + i] * 2 + ids[1]], give.at[i], sems.at[i])
        for i in range(give.shape[0])
    ]
    for copy in copies:
        copy.start()
    for copy in copies:
        copy.wait()


def pick(plan, ids, waves, pools, cap, chunk):
    shift, first, count = chunk
    return pl.pallas_call(
        functools.partial(pick_kernel, (2 * pools + shift) * cap + first),
        out_shape=jax.ShapeDtypeStruct((count,) + waves.shape[1:], waves.dtype),
        in_specs=[SMEM, SMEM, ANY],
        out_specs=pl.BlockSpec(memory_space=pltpu.VMEM),
        scratch_shapes=[pltpu.SemaphoreType.DMA((count,))],
        compiler_params=PARAMS,
        cost_estimate=LIGHT,
        name="pick",
    )(plan, ids, waves)


def to_real(own, other, table, z_points):
    stacked = 2 * z_points
    bands = own.shape[1]
    parts = [[], [], [], []]
    for c in range(own.shape[0] // stacked):
        rows = slice(c * stacked, (c + 1) * stacked)
        pair = jnp.concatenate([own[rows], other[rows]], axis=1)
        out = jnp.dot(table, pair, preferred_element_type=F32)
        parts[0].append(out[:z_points, :bands])
        parts[1].append(out[z_points:, :bands])
        parts[2].append(out[:z_points, bands:])
        parts[3].append(out[z_points:, bands:])
    return [jnp.concatenate(part, axis=0).astype(BF16) for part in parts]


def piece_of(count):
    return max(1, count // 2)


def couple_kernel(shape, plan, ids, table, pots, own, other, keep, *rest):
    number, first, size, groups, z_points = shape
    gives, hold = rest[:-1], rest[-1]

    @pl.when(first + pl.program_id(0) < plan[number])
    def _():
        own_re, own_im, o_re, o_im = to_real(own[0], other[0], table[...], z_points)
        u_re, u_im = own_re.astype(F32), own_im.astype(F32)
        both_o = jnp.concatenate([o_re, o_im], axis=1).T
        bands = o_re.shape[1]
        share = bands // groups
        mine = pots.shape[0] // 2
        starts = [
            pl.multiple_of(lax.rem(g - ids[2] + groups, groups) * share, share)
            for g in range(groups)
        ]
        for j in range(2 * mine):
            p_re, p_im = pots[j, 0], pots[j, 1]
            w_re = (p_re * u_re - p_im * u_im).astype(BF16)
            w_im = (p_re * u_im + p_im * u_re).astype(BF16)
            both = jnp.dot(
                both_o, jnp.concatenate([w_re, w_im], axis=1), preferred_element_type=F32
            )
            real = both[:bands, :bands] + both[bands:, bands:]
            imag = both[:bands, bands:] - both[bands:, :bands]
            for part, value in ((0, real), (1, imag)):
                for g in range(groups):
                    rows = value[g * share : (g + 1) * share]
                    if j < mine:
                        keep[0, 2 * j + part, pl.ds(starts[g], share), :] = rows
                    else:
                        place = 2 * (j - mine) + part
                        hold[place, pl.ds(starts[g], share), :] = rows.astype(BF16)

        for at, give in enumerate(gives):

            @pl.when(pl.program_id(0) // size == at)
            def _(give=give):
                give[0] = hold[...]


def couple(plan, ids, table, pots, waves, other, chunk, pools, cap, groups):
    shift, first, count = chunk
    half, bands = waves.shape[1:]
    parts = pots.shape[0]
    base = shift * cap + first
    block = (1, half, bands)
    own_block = pl.BlockSpec(block, lambda i, plan, ids: (plan[base + i] * 2 + ids[1], 0, 0))
    if shift == 0:
        other_block = pl.BlockSpec(
            block, lambda i, plan, ids: (plan[pools * cap + base + i] * 2 + ids[1], 0, 0)
        )
    else:
        other_block = pl.BlockSpec(block, lambda i, plan, ids: (i, 0, 0))
    out_block = (1, parts, bands, bands)
    size = piece_of(count)
    pieces = [(at, min(size, count - at)) for at in range(0, count, size)]
    shape = (3 * pools * cap + shift, first, size, groups, table.shape[0] // 2)
    return pl.pallas_call(
        functools.partial(couple_kernel, shape),
        grid_spec=pltpu.PrefetchScalarGridSpec(
            num_scalar_prefetch=2,
            grid=(count,),
            in_specs=[
                pl.BlockSpec(table.shape, lambda i, plan, ids: (0, 0)),
                pl.BlockSpec(pots.shape, lambda i, plan, ids: (0, 0, 0, 0)),
                own_block, other_block,
            ],
            out_specs=[pl.BlockSpec(out_block, lambda i, plan, ids: (i, 0, 0, 0))] + [
                pl.BlockSpec(
                    out_block,
                    lambda i, plan, ids, at=at, size=size: (jnp.clip(i - at, 0, size - 1), 0, 0, 0),
                )
                for at, size in pieces
            ],
            scratch_shapes=[pltpu.VMEM((parts, bands, bands), BF16)],
        ),
        out_shape=[jax.ShapeDtypeStruct((count, parts, bands, bands), F32)] + [
            jax.ShapeDtypeStruct((size, parts, bands, bands), BF16) for _, size in pieces
        ],
        compiler_params=PARAMS,
        cost_estimate=LIGHT,
        name="couple",
    )(plan, ids, table, pots, waves, other)


def combine_kernel(shapes, others, scaling, plan, *refs):
    result, stage, sems = refs[-3:]
    terms = list(refs[-3 - sum(1 + shape[4] + others for shape in shapes) : -3])
    blocks = []
    for number, base, first, count, pieces in shapes:
        kept = terms.pop(0)
        added = [([terms.pop(0) for _ in range(pieces)], piece_of(count))]
        added += [([terms.pop(0)], count) for _ in range(others)]
        for i in range(count):
            blocks.append((number, base + i, first + i, kept, added, i))

    def each(action):
        for at, (number, entry, slot, kept, added, i) in enumerate(blocks):

            @pl.when(slot < plan[number])
            def _(at=at, entry=entry, kept=kept, added=added, i=i):
                copy = pltpu.make_async_copy(stage.at[at], result.at[plan[entry]], sems.at[at])
                action(at, copy, kept, added, i)

    def add(at, copy, kept, added, i):
        value = kept[i]
        for pieces, size in added:
            value = value + pieces[i // size][i % size].astype(F32)
        stage[at] = (value * scaling).astype(BF16)
        copy.start()

    each(add)
    each(lambda at, copy, kept, added, i: copy.wait())


def combine(plan, before, parcels, local_k, pools, cap, scaling):
    terms, shapes, total = [], [], 0
    for (shift, first, count), kept, got, arrived in parcels:
        terms += [kept, *got, *arrived]
        shapes.append((3 * pools * cap + shift, shift * cap + first, first, count, len(got)))
        total += count
        others = len(arrived)
        parts, share, bands = arrived[0].shape[1:]
    blocks = [
        pl.BlockSpec((term.shape[0], parts, share, bands), lambda i, plan: (0, 0, 0, 0))
        for term in terms
    ]
    operands = ([] if before is None else [before]) + terms
    return pl.pallas_call(
        functools.partial(combine_kernel, shapes, others, scaling),
        grid_spec=pltpu.PrefetchScalarGridSpec(
            num_scalar_prefetch=1,
            grid=(1,),
            in_specs=([] if before is None else [ANY]) + blocks,
            out_specs=ANY,
            scratch_shapes=[
                pltpu.VMEM((total, parts, share, bands), BF16),
                pltpu.SemaphoreType.DMA((total,)),
            ],
        ),
        out_shape=jax.ShapeDtypeStruct((local_k, parts, share, bands), BF16),
        input_output_aliases={} if before is None else {1: 0},
        compiler_params=PARAMS,
        cost_estimate=LIGHT,
        name="combine",
    )(plan, *operands)


def after(value, *others):
    return lax.optimization_barrier((value, *others))[0]


def transfers(pools, cap):
    moves = []
    for s in range(1, (pools + 1) // 2):
        moves += [(s, 0, cap), (pools - s, 0, cap)]
    if pools % 2 == 0:
        large = (3 * cap + 2) // 5
        moves += [(pools // 2, 0, large), (pools // 2, large, cap - large)]
    waits = [i - WINDOW if i >= WINDOW else None for i in range(len(moves))]
    return moves, waits


def body(wavefunctions, potentials, pert_order, partners):
    local_k, columns, stacked, bands = wavefunctions.shape
    z_points = stacked // 2
    pools = lax.axis_size("pool")
    groups = lax.axis_size("ga")
    cores = lax.axis_size("pert")
    my_pool = lax.axis_index("pool")
    my_core = lax.axis_index("pert")
    my_group = lax.axis_index("ga")
    cap = max(2, local_k // pools + 1)
    half = columns // cores
    share = bands // groups
    ids = jnp.stack([my_pool, my_core, my_group]).astype(jnp.int32)
    waves = wavefunctions.reshape(local_k * cores, half * stacked, bands)
    swap_cores = [(c, cores - 1 - c) for c in range(cores)]

    plan = make_plan(ids, partners, pools, local_k, cap)
    moves, waits = transfers(pools, cap)
    gives = [pick(plan, ids, waves, pools, cap, move) for move in moves]
    potentials = after(potentials, gives[0])

    per_device = potentials.shape[0]
    by_half = potentials.reshape(per_device, cores, half, stacked)
    mine_now = lax.dynamic_index_in_dim(by_half, my_core, 1, keepdims=False)
    theirs_now = lax.dynamic_index_in_dim(by_half, 1 - my_core, 1, keepdims=False)
    other_pots = lax.ppermute(theirs_now, "pert", swap_cores)
    ordered = jnp.roll(pert_order.reshape(cores, per_device), -my_core, axis=0).reshape(-1)
    stored = jnp.where(
        my_core == 0, jnp.stack([mine_now, other_pots]), jnp.stack([other_pots, mine_now])
    ).reshape((cores * per_device,) + mine_now.shape[1:])
    options = jnp.arange(cores * per_device, dtype=jnp.int32)
    chosen = jnp.sum(
        jnp.where(
            (ordered[:, None] == options[None, :])[:, :, None, None], stored[None],
            jnp.zeros((), F32),
        ),
        axis=1,
    ).reshape(cores * per_device, half, 2, z_points)
    pots = jnp.moveaxis(chosen, 2, 1).reshape(cores * per_device, 2, half * z_points, 1)
    pots = jnp.broadcast_to(pots, pots.shape[:3] + (bands,))
    table = dft_table(z_points)
    scaling = 1.0 / math.sqrt(columns * groups * z_points)

    landed = []
    for move, wait, give in zip(moves, waits, gives):
        if wait is not None:
            give = after(give, landed[wait])
        pairs = [(p, (p + move[0]) % pools) for p in range(pools)]
        landed.append(lax.ppermute(give, "pool", pairs))

    chunks = [((0, 0, cap), waves), *zip(moves, landed)]
    kept, got, terms = [], [], []
    result = None

    def exchange(i):
        sent = []
        size = piece_of(kept[i].shape[0])
        for step in range(1, groups):
            rows = slice(step * share, (step + 1) * share)
            pairs = [(g, (g + step) % groups) for g in range(groups)]
            total = jnp.concatenate(
                [
                    kept[i][at * size : at * size + piece.shape[0], :, rows]
                    + piece[:, :, rows].astype(F32)
                    for at, piece in enumerate(got[i])
                ],
                axis=0,
            )
            sent.append(lax.ppermute(total.astype(BF16), "ga", pairs))
        terms.append(sent)

    finished = 0

    def finish(until, result):
        parcels = [(chunks[i][0], kept[i], got[i], terms[i]) for i in range(finished, until)]
        return combine(plan, result, parcels, local_k, pools, cap, scaling)

    last = len(chunks) - 1
    for i, (chunk, other) in enumerate(chunks):
        if i >= 1:
            other = after(other, kept[i - 1])
        if i >= LAG_CORE:
            exchange(i - LAG_CORE)
            other = after(other, *got[i - LAG_CORE])
        if i >= LAG_GROUP:
            other = after(other, *terms[i - LAG_GROUP])
        if last - i in COMBINE and i - LAG_GROUP + 1 > finished:
            result = finish(i - LAG_GROUP + 1, result)
            finished = i - LAG_GROUP + 1
            other = after(other, result)
        keep, *gives_now = couple(plan, ids, table, pots, waves, other, chunk, pools, cap, groups)
        kept.append(keep)
        got.append([lax.ppermute(give, "pert", swap_cores) for give in gives_now])
    for i in range(len(terms), len(chunks)):
        exchange(i)
    result = finish(len(chunks), result)
    return result.reshape(local_k, per_device, 2, share, bands)


LAG_CORE, LAG_GROUP = 1, 2
WINDOW = 2
COMBINE = (1,)


def solution(mesh):
    return jax.shard_map(
        body,
        mesh=mesh,
        in_specs=(P("pool", "ga", None, None), P(("pb", "pert"), "ga", None), P(), P("pb")),
        out_specs=P(("pb", "pool"), "pert", None, "ga", None),
        check_vma=False,
    )
```

```python
import functools
import math

import jax
import jax.numpy as jnp
from jax import lax
from jax.experimental import pallas as pl
from jax.experimental.pallas import tpu as pltpu
from jax.sharding import PartitionSpec as P

BF16 = jnp.bfloat16
F32 = jnp.float32
ANY = pl.BlockSpec(memory_space=pl.ANY)
SMEM = pl.BlockSpec(memory_space=pltpu.SMEM)
VMEM_LIMIT = 60 * 1024 * 1024
LIGHT = pl.CostEstimate(flops=1, bytes_accessed=1024, transcendentals=0)
PARAMS = pltpu.CompilerParams(vmem_limit_bytes=VMEM_LIMIT)


def dft_table(length):
    positions = jnp.arange(length, dtype=jnp.int32)
    product = positions[:, None] * positions[None, :] % length
    angles = product.astype(F32) * (2.0 * math.pi / length)
    cosine = jnp.cos(angles) / math.sqrt(length)
    sine_part = jnp.sin(angles) / math.sqrt(length)
    upper_rows = jnp.concatenate([cosine, -sine_part], axis=1)
    bottom = jnp.concatenate([sine_part, cosine], axis=1)
    return jnp.concatenate([upper_rows, bottom], axis=0).astype(BF16)


def plan_kernel(pools, local_k, cap, ids, partners, plan):
    me = ids[0]
    size = pools * cap
    counts = 3 * size

    def clear(i, carry):
        plan[i] = 0
        return carry

    lax.fori_loop(0, counts + pools, clear, 0, unroll=8)

    def visit(t, tally):
        want = partners[me * local_k + t]
        holder = lax.div(want, local_k)
        shift = lax.rem(me - holder + pools, pools)
        slot = plan[counts + shift]
        plan[shift * cap + slot] = t
        plan[size + shift * cap + slot] = want - holder * local_k
        plan[counts + shift] = slot + 1
        after = []
        for shift in range(1, pools):
            taker = lax.rem(me + shift, pools)
            want = partners[taker * local_k + t]
            slot = tally[shift - 1]
            mine = lax.div(want, local_k) == me
            entry = 2 * size + shift * cap + jnp.minimum(slot, cap - 1)
            plan[entry] = jnp.where(mine, lax.rem(want, local_k), plan[entry])
            after.append(slot + mine.astype(jnp.int32))
        return tuple(after)

    lax.fori_loop(0, local_k, visit, (jnp.int32(0),) * (pools - 1), unroll=2)


def make_plan(ids, partners, pools, local_k, cap):
    return pl.pallas_call(
        functools.partial(plan_kernel, pools, local_k, cap),
        out_shape=jax.ShapeDtypeStruct((3 * pools * cap + pools,), jnp.int32),
        in_specs=[SMEM, SMEM],
        out_specs=SMEM,
        cost_estimate=LIGHT,
        name="plan",
    )(ids, partners)


def pick_kernel(base, plan, ids, waves, give, sems):
    copies = [
        pltpu.make_async_copy(waves.at[plan[base + i] * 2 + ids[1]], give.at[i], sems.at[i])
        for i in range(give.shape[0])
    ]
    for copy in copies:
        copy.start()
    for copy in copies:
        copy.wait()


def pick(plan, ids, waves, pools, cap, chunk):
    shift, first, count = chunk
    return pl.pallas_call(
        functools.partial(pick_kernel, (2 * pools + shift) * cap + first),
        out_shape=jax.ShapeDtypeStruct((count,) + waves.shape[1:], waves.dtype),
        in_specs=[SMEM, SMEM, ANY],
        out_specs=pl.BlockSpec(memory_space=pltpu.VMEM),
        scratch_shapes=[pltpu.SemaphoreType.DMA((count,))],
        compiler_params=PARAMS,
        cost_estimate=LIGHT,
        name="pick",
    )(plan, ids, waves)


def to_real(own, other, table, z_points):
    stacked = 2 * z_points
    bands = own.shape[1]
    parts = [[], [], [], []]
    for c in range(own.shape[0] // stacked):
        rows = slice(c * stacked, (c + 1) * stacked)
        pair = jnp.concatenate([own[rows], other[rows]], axis=1)
        out = jnp.dot(table, pair, preferred_element_type=F32)
        parts[0].append(out[:z_points, :bands])
        parts[1].append(out[z_points:, :bands])
        parts[2].append(out[:z_points, bands:])
        parts[3].append(out[z_points:, bands:])
    return [jnp.concatenate(part, axis=0).astype(BF16) for part in parts]


def piece_of(count):
    return max(1, count // 2)


def couple_kernel(shape, plan, ids, table, pots, own, other, keep, *rest):
    number, first, size, groups, z_points = shape
    gives, hold = rest[:-1], rest[-1]

    @pl.when(first + pl.program_id(0) < plan[number])
    def _():
        own_re, own_im, o_re, o_im = to_real(own[0], other[0], table[...], z_points)
        u_re, u_im = own_re.astype(F32), own_im.astype(F32)
        both_o = jnp.concatenate([o_re, o_im], axis=1).T
        bands = o_re.shape[1]
        share = bands // groups
        mine = pots.shape[0] // 2
        starts = [
            pl.multiple_of(lax.rem(g - ids[2] + groups, groups) * share, share)
            for g in range(groups)
        ]
        for j in range(2 * mine):
            p_re, p_im = pots[j, 0], pots[j, 1]
            w_re = (p_re * u_re - p_im * u_im).astype(BF16)
            w_im = (p_re * u_im + p_im * u_re).astype(BF16)
            both = jnp.dot(
                both_o, jnp.concatenate([w_re, w_im], axis=1), preferred_element_type=F32
            )
            real = both[:bands, :bands] + both[bands:, bands:]
            imag = both[:bands, bands:] - both[bands:, :bands]
            for part, value in ((0, real), (1, imag)):
                for g in range(groups):
                    rows = value[g * share : (g + 1) * share]
                    if j < mine:
                        keep[0, 2 * j + part, pl.ds(starts[g], share), :] = rows
                    else:
                        place = 2 * (j - mine) + part
                        hold[place, pl.ds(starts[g], share), :] = rows.astype(BF16)

        for at, give in enumerate(gives):

            @pl.when(pl.program_id(0) // size == at)
            def _(give=give):
                give[0] = hold[...]


def couple(plan, ids, table, pots, waves, other, chunk, pools, cap, groups):
    shift, first, count = chunk
    half, bands = waves.shape[1:]
    parts = pots.shape[0]
    base = shift * cap + first
    block = (1, half, bands)
    own_block = pl.BlockSpec(block, lambda i, plan, ids: (plan[base + i] * 2 + ids[1], 0, 0))
    if shift == 0:
        other_block = pl.BlockSpec(
            block, lambda i, plan, ids: (plan[pools * cap + base + i] * 2 + ids[1], 0, 0)
        )
    else:
        other_block = pl.BlockSpec(block, lambda i, plan, ids: (i, 0, 0))
    out_block = (1, parts, bands, bands)
    size = piece_of(count)
    pieces = [(at, min(size, count - at)) for at in range(0, count, size)]
    shape = (3 * pools * cap + shift, first, size, groups, table.shape[0] // 2)
    return pl.pallas_call(
        functools.partial(couple_kernel, shape),
        grid_spec=pltpu.PrefetchScalarGridSpec(
            num_scalar_prefetch=2,
            grid=(count,),
            in_specs=[
                pl.BlockSpec(table.shape, lambda i, plan, ids: (0, 0)),
                pl.BlockSpec(pots.shape, lambda i, plan, ids: (0, 0, 0, 0)),
                own_block, other_block,
            ],
            out_specs=[pl.BlockSpec(out_block, lambda i, plan, ids: (i, 0, 0, 0))] + [
                pl.BlockSpec(
                    out_block,
                    lambda i, plan, ids, at=at, size=size: (jnp.clip(i - at, 0, size - 1), 0, 0, 0),
                )
                for at, size in pieces
            ],
            scratch_shapes=[pltpu.VMEM((parts, bands, bands), BF16)],
        ),
        out_shape=[jax.ShapeDtypeStruct((count, parts, bands, bands), F32)] + [
            jax.ShapeDtypeStruct((size, parts, bands, bands), BF16) for _, size in pieces
        ],
        compiler_params=PARAMS,
        cost_estimate=LIGHT,
        name="couple",
    )(plan, ids, table, pots, waves, other)


def combine_kernel(shapes, others, scaling, plan, *refs):
    result, stage, sems = refs[-3:]
    terms = list(refs[-3 - sum(1 + shape[4] + others for shape in shapes) : -3])
    blocks = []
    for number, base, first, count, pieces in shapes:
        kept = terms.pop(0)
        added = [([terms.pop(0) for _ in range(pieces)], piece_of(count))]
        added += [([terms.pop(0)], count) for _ in range(others)]
        for i in range(count):
            blocks.append((number, base + i, first + i, kept, added, i))

    def each(action):
        for at, (number, entry, slot, kept, added, i) in enumerate(blocks):

            @pl.when(slot < plan[number])
            def _(at=at, entry=entry, kept=kept, added=added, i=i):
                copy = pltpu.make_async_copy(stage.at[at], result.at[plan[entry]], sems.at[at])
                action(at, copy, kept, added, i)

    def add(at, copy, kept, added, i):
        value = kept[i]
        for pieces, size in added:
            value = value + pieces[i // size][i % size].astype(F32)
        stage[at] = (value * scaling).astype(BF16)
        copy.start()

    each(add)
    each(lambda at, copy, kept, added, i: copy.wait())


def combine(plan, before, parcels, local_k, pools, cap, scaling):
    terms, shapes, total = [], [], 0
    for (shift, first, count), kept, got, arrived in parcels:
        terms += [kept, *got, *arrived]
        shapes.append((3 * pools * cap + shift, shift * cap + first, first, count, len(got)))
        total += count
        others = len(arrived)
        parts, share, bands = arrived[0].shape[1:]
    blocks = [
        pl.BlockSpec((term.shape[0], parts, share, bands), lambda i, plan: (0, 0, 0, 0))
        for term in terms
    ]
    operands = ([] if before is None else [before]) + terms
    return pl.pallas_call(
        functools.partial(combine_kernel, shapes, others, scaling),
        grid_spec=pltpu.PrefetchScalarGridSpec(
            num_scalar_prefetch=1,
            grid=(1,),
            in_specs=([] if before is None else [ANY]) + blocks,
            out_specs=ANY,
            scratch_shapes=[
                pltpu.VMEM((total, parts, share, bands), BF16),
                pltpu.SemaphoreType.DMA((total,)),
            ],
        ),
        out_shape=jax.ShapeDtypeStruct((local_k, parts, share, bands), BF16),
        input_output_aliases={} if before is None else {1: 0},
        compiler_params=PARAMS,
        cost_estimate=LIGHT,
        name="combine",
    )(plan, *operands)


def after(value, *others):
    return lax.optimization_barrier((value, *others))[0]


def transfers(pools, cap):
    moves = []
    for s in range(1, (pools + 1) // 2):
        moves += [(s, 0, cap), (pools - s, 0, cap)]
    if pools % 2 == 0:
        large = (3 * cap + 2) // 5
        moves += [(pools // 2, 0, large), (pools // 2, large, cap - large)]
    waits = [None] + [max(0, i - 2) for i in range(1, len(moves))]
    return moves, waits


def body(wavefunctions, potentials, pert_order, partners):
    local_k, columns, stacked, bands = wavefunctions.shape
    z_points = stacked // 2
    pools = lax.axis_size("pool")
    groups = lax.axis_size("ga")
    cores = lax.axis_size("pert")
    my_pool = lax.axis_index("pool")
    my_core = lax.axis_index("pert")
    my_group = lax.axis_index("ga")
    cap = max(2, local_k // pools + 1)
    half = columns // cores
    share = bands // groups
    ids = jnp.stack([my_pool, my_core, my_group]).astype(jnp.int32)
    waves = wavefunctions.reshape(local_k * cores, half * stacked, bands)
    swap_cores = [(c, cores - 1 - c) for c in range(cores)]

    plan = make_plan(ids, partners, pools, local_k, cap)
    moves, waits = transfers(pools, cap)
    gives = [pick(plan, ids, waves, pools, cap, move) for move in moves]
    potentials = after(potentials, gives[0])

    per_device = potentials.shape[0]
    by_half = potentials.reshape(per_device, cores, half, stacked)
    mine_now = lax.dynamic_index_in_dim(by_half, my_core, 1, keepdims=False)
    theirs_now = lax.dynamic_index_in_dim(by_half, 1 - my_core, 1, keepdims=False)
    other_pots = lax.ppermute(theirs_now, "pert", swap_cores)
    ordered = jnp.roll(pert_order.reshape(cores, per_device), -my_core, axis=0).reshape(-1)
    stored = jnp.where(
        my_core == 0, jnp.stack([mine_now, other_pots]), jnp.stack([other_pots, mine_now])
    ).reshape((cores * per_device,) + mine_now.shape[1:])
    options = jnp.arange(cores * per_device, dtype=jnp.int32)
    chosen = jnp.sum(
        jnp.where(
            (ordered[:, None] == options[None, :])[:, :, None, None], stored[None],
            jnp.zeros((), F32),
        ),
        axis=1,
    ).reshape(cores * per_device, half, 2, z_points)
    pots = jnp.moveaxis(chosen, 2, 1).reshape(cores * per_device, 2, half * z_points, 1)
    pots = jnp.broadcast_to(pots, pots.shape[:3] + (bands,))
    table = dft_table(z_points)
    scaling = 1.0 / math.sqrt(columns * groups * z_points)

    landed = []
    for move, wait, give in zip(moves, waits, gives):
        if wait is not None:
            give = after(give, landed[wait])
        pairs = [(p, (p + move[0]) % pools) for p in range(pools)]
        landed.append(lax.ppermute(give, "pool", pairs))

    chunks = [((0, 0, cap), waves), *zip(moves, landed)]
    kept, got, terms = [], [], []
    result = None

    def exchange(i):
        sent = []
        size = piece_of(kept[i].shape[0])
        for step in range(1, groups):
            rows = slice(step * share, (step + 1) * share)
            pairs = [(g, (g + step) % groups) for g in range(groups)]
            total = jnp.concatenate(
                [
                    kept[i][at * size : at * size + piece.shape[0], :, rows]
                    + piece[:, :, rows].astype(F32)
                    for at, piece in enumerate(got[i])
                ],
                axis=0,
            )
            sent.append(lax.ppermute(total.astype(BF16), "ga", pairs))
        terms.append(sent)

    finished = 0

    def finish(until, result):
        parcels = [(chunks[i][0], kept[i], got[i], terms[i]) for i in range(finished, until)]
        return combine(plan, result, parcels, local_k, pools, cap, scaling)

    last = len(chunks) - 1
    for i, (chunk, other) in enumerate(chunks):
        if i >= 1:
            other = after(other, kept[i - 1])
        if i >= LAG_CORE:
            exchange(i - LAG_CORE)
            other = after(other, *got[i - LAG_CORE])
        if i >= LAG_GROUP:
            other = after(other, *terms[i - LAG_GROUP])
        if last - i in COMBINE and i - LAG_GROUP + 1 > finished:
            result = finish(i - LAG_GROUP + 1, result)
            finished = i - LAG_GROUP + 1
            other = after(other, result)
        keep, *gives_now = couple(plan, ids, table, pots, waves, other, chunk, pools, cap, groups)
        kept.append(keep)
        got.append([lax.ppermute(give, "pert", swap_cores) for give in gives_now])
    for i in range(len(terms), len(chunks)):
        exchange(i)
    result = finish(len(chunks), result)
    return result.reshape(local_k, per_device, 2, share, bands)


LAG_CORE, LAG_GROUP = 1, 2
COMBINE = (1,)


def solution(mesh):
    return jax.shard_map(
        body,
        mesh=mesh,
        in_specs=(P("pool", "ga", None, None), P(("pb", "pert"), "ga", None), P(), P("pb")),
        out_specs=P(("pb", "pool"), "pert", None, "ga", None),
        check_vma=False,
    )
```

```python
import functools
import math

import jax
import jax.numpy as jnp
from jax import lax
from jax.experimental import pallas as pl
from jax.experimental.pallas import tpu as pltpu
from jax.sharding import PartitionSpec as P

BF16 = jnp.bfloat16
F32 = jnp.float32
ANY = pl.BlockSpec(memory_space=pl.ANY)
SMEM = pl.BlockSpec(memory_space=pltpu.SMEM)
VMEM_LIMIT = 60 * 1024 * 1024
LIGHT = pl.CostEstimate(flops=1, bytes_accessed=1024, transcendentals=0)
PARAMS = pltpu.CompilerParams(vmem_limit_bytes=VMEM_LIMIT)


def dft_table(length):
    positions = jnp.arange(length, dtype=jnp.int32)
    product = positions[:, None] * positions[None, :] % length
    angles = product.astype(F32) * (2.0 * math.pi / length)
    cosine = jnp.cos(angles) / math.sqrt(length)
    sine_part = jnp.sin(angles) / math.sqrt(length)
    upper_rows = jnp.concatenate([cosine, -sine_part], axis=1)
    bottom = jnp.concatenate([sine_part, cosine], axis=1)
    return jnp.concatenate([upper_rows, bottom], axis=0).astype(BF16)


def plan_kernel(pools, local_k, cap, ids, partners, plan):
    me = ids[0]
    size = pools * cap
    counts = 3 * size

    def clear(i, carry):
        plan[i] = 0
        return carry

    lax.fori_loop(0, counts + pools, clear, 0, unroll=8)

    def visit(t, tally):
        want = partners[me * local_k + t]
        holder = lax.div(want, local_k)
        shift = lax.rem(me - holder + pools, pools)
        slot = plan[counts + shift]
        plan[shift * cap + slot] = t
        plan[size + shift * cap + slot] = want - holder * local_k
        plan[counts + shift] = slot + 1
        after = []
        for shift in range(1, pools):
            taker = lax.rem(me + shift, pools)
            want = partners[taker * local_k + t]
            slot = tally[shift - 1]
            mine = lax.div(want, local_k) == me
            entry = 2 * size + shift * cap + jnp.minimum(slot, cap - 1)
            plan[entry] = jnp.where(mine, lax.rem(want, local_k), plan[entry])
            after.append(slot + mine.astype(jnp.int32))
        return tuple(after)

    lax.fori_loop(0, local_k, visit, (jnp.int32(0),) * (pools - 1), unroll=2)


def make_plan(ids, partners, pools, local_k, cap):
    return pl.pallas_call(
        functools.partial(plan_kernel, pools, local_k, cap),
        out_shape=jax.ShapeDtypeStruct((3 * pools * cap + pools,), jnp.int32),
        in_specs=[SMEM, SMEM],
        out_specs=SMEM,
        cost_estimate=LIGHT,
        name="plan",
    )(ids, partners)


def pick_kernel(base, plan, ids, waves, give, sems):
    copies = [
        pltpu.make_async_copy(waves.at[plan[base + i] * 2 + ids[1]], give.at[i], sems.at[i])
        for i in range(give.shape[0])
    ]
    for copy in copies:
        copy.start()
    for copy in copies:
        copy.wait()


def pick(plan, ids, waves, pools, cap, chunk):
    shift, first, count = chunk
    return pl.pallas_call(
        functools.partial(pick_kernel, (2 * pools + shift) * cap + first),
        out_shape=jax.ShapeDtypeStruct((count,) + waves.shape[1:], waves.dtype),
        in_specs=[SMEM, SMEM, ANY],
        out_specs=pl.BlockSpec(memory_space=pltpu.VMEM),
        scratch_shapes=[pltpu.SemaphoreType.DMA((count,))],
        compiler_params=PARAMS,
        cost_estimate=LIGHT,
        name="pick",
    )(plan, ids, waves)


def to_real(own, other, table, z_points):
    stacked = 2 * z_points
    bands = own.shape[1]
    parts = [[], [], [], []]
    for c in range(own.shape[0] // stacked):
        rows = slice(c * stacked, (c + 1) * stacked)
        pair = jnp.concatenate([own[rows], other[rows]], axis=1)
        out = jnp.dot(table, pair, preferred_element_type=F32)
        parts[0].append(out[:z_points, :bands])
        parts[1].append(out[z_points:, :bands])
        parts[2].append(out[:z_points, bands:])
        parts[3].append(out[z_points:, bands:])
    return [jnp.concatenate(part, axis=0).astype(BF16) for part in parts]


def piece_of(count):
    return 1 if count < 5 else 2


def couple_kernel(shape, plan, ids, table, pots, own, other, keep, *rest):
    number, first, size, groups, z_points = shape
    gives, hold = rest[:-1], rest[-1]

    @pl.when(first + pl.program_id(0) < plan[number])
    def _():
        own_re, own_im, o_re, o_im = to_real(own[0], other[0], table[...], z_points)
        u_re, u_im = own_re.astype(F32), own_im.astype(F32)
        both_o = jnp.concatenate([o_re, o_im], axis=1).T
        bands = o_re.shape[1]
        share = bands // groups
        mine = pots.shape[0] // 2
        starts = [
            pl.multiple_of(lax.rem(g - ids[2] + groups, groups) * share, share)
            for g in range(groups)
        ]
        for j in range(2 * mine):
            p_re, p_im = pots[j, 0], pots[j, 1]
            w_re = (p_re * u_re - p_im * u_im).astype(BF16)
            w_im = (p_re * u_im + p_im * u_re).astype(BF16)
            both = jnp.dot(
                both_o, jnp.concatenate([w_re, w_im], axis=1), preferred_element_type=F32
            )
            real = both[:bands, :bands] + both[bands:, bands:]
            imag = both[:bands, bands:] - both[bands:, :bands]
            for part, value in ((0, real), (1, imag)):
                for g in range(groups):
                    rows = value[g * share : (g + 1) * share]
                    if j < mine:
                        keep[0, 2 * j + part, pl.ds(starts[g], share), :] = rows
                    else:
                        place = 2 * (j - mine) + part
                        hold[place, pl.ds(starts[g], share), :] = rows.astype(BF16)

        for at, give in enumerate(gives):

            @pl.when(pl.program_id(0) // size == at)
            def _(give=give):
                give[0] = hold[...]


def couple(plan, ids, table, pots, waves, other, chunk, pools, cap, groups):
    shift, first, count = chunk
    half, bands = waves.shape[1:]
    parts = pots.shape[0]
    base = shift * cap + first
    block = (1, half, bands)
    own_block = pl.BlockSpec(block, lambda i, plan, ids: (plan[base + i] * 2 + ids[1], 0, 0))
    if shift == 0:
        other_block = pl.BlockSpec(
            block, lambda i, plan, ids: (plan[pools * cap + base + i] * 2 + ids[1], 0, 0)
        )
    else:
        other_block = pl.BlockSpec(block, lambda i, plan, ids: (i, 0, 0))
    out_block = (1, parts, bands, bands)
    size = piece_of(count)
    pieces = [(at, min(size, count - at)) for at in range(0, count, size)]
    shape = (3 * pools * cap + shift, first, size, groups, table.shape[0] // 2)
    return pl.pallas_call(
        functools.partial(couple_kernel, shape),
        grid_spec=pltpu.PrefetchScalarGridSpec(
            num_scalar_prefetch=2,
            grid=(count,),
            in_specs=[
                pl.BlockSpec(table.shape, lambda i, plan, ids: (0, 0)),
                pl.BlockSpec(pots.shape, lambda i, plan, ids: (0, 0, 0, 0)),
                own_block, other_block,
            ],
            out_specs=[pl.BlockSpec(out_block, lambda i, plan, ids: (i, 0, 0, 0))] + [
                pl.BlockSpec(
                    out_block,
                    lambda i, plan, ids, at=at, size=size: (jnp.clip(i - at, 0, size - 1), 0, 0, 0),
                )
                for at, size in pieces
            ],
            scratch_shapes=[pltpu.VMEM((parts, bands, bands), BF16)],
        ),
        out_shape=[jax.ShapeDtypeStruct((count, parts, bands, bands), F32)] + [
            jax.ShapeDtypeStruct((size, parts, bands, bands), BF16) for _, size in pieces
        ],
        compiler_params=PARAMS,
        cost_estimate=LIGHT,
        name="couple",
    )(plan, ids, table, pots, waves, other)


def combine_kernel(shapes, others, scaling, plan, *refs):
    result, stage, sems = refs[-3:]
    terms = list(refs[-3 - sum(1 + shape[4] + others for shape in shapes) : -3])
    blocks = []
    for number, base, first, count, pieces in shapes:
        kept = terms.pop(0)
        added = [([terms.pop(0) for _ in range(pieces)], piece_of(count))]
        added += [([terms.pop(0)], count) for _ in range(others)]
        for i in range(count):
            blocks.append((number, base + i, first + i, kept, added, i))

    def each(action):
        for at, (number, entry, slot, kept, added, i) in enumerate(blocks):

            @pl.when(slot < plan[number])
            def _(at=at, entry=entry, kept=kept, added=added, i=i):
                copy = pltpu.make_async_copy(stage.at[at], result.at[plan[entry]], sems.at[at])
                action(at, copy, kept, added, i)

    def add(at, copy, kept, added, i):
        value = kept[i]
        for pieces, size in added:
            value = value + pieces[i // size][i % size].astype(F32)
        stage[at] = (value * scaling).astype(BF16)
        copy.start()

    each(add)
    each(lambda at, copy, kept, added, i: copy.wait())


def combine(plan, before, parcels, local_k, pools, cap, scaling):
    terms, shapes, total = [], [], 0
    for (shift, first, count), kept, got, arrived in parcels:
        terms += [kept, *got, *arrived]
        shapes.append((3 * pools * cap + shift, shift * cap + first, first, count, len(got)))
        total += count
        others = len(arrived)
        parts, share, bands = arrived[0].shape[1:]
    blocks = [
        pl.BlockSpec((term.shape[0], parts, share, bands), lambda i, plan: (0, 0, 0, 0))
        for term in terms
    ]
    operands = ([] if before is None else [before]) + terms
    return pl.pallas_call(
        functools.partial(combine_kernel, shapes, others, scaling),
        grid_spec=pltpu.PrefetchScalarGridSpec(
            num_scalar_prefetch=1,
            grid=(1,),
            in_specs=([] if before is None else [ANY]) + blocks,
            out_specs=ANY,
            scratch_shapes=[
                pltpu.VMEM((total, parts, share, bands), BF16),
                pltpu.SemaphoreType.DMA((total,)),
            ],
        ),
        out_shape=jax.ShapeDtypeStruct((local_k, parts, share, bands), BF16),
        input_output_aliases={} if before is None else {1: 0},
        compiler_params=PARAMS,
        cost_estimate=LIGHT,
        name="combine",
    )(plan, *operands)


def after(value, *others):
    return lax.optimization_barrier((value, *others))[0]


def transfers(pools, cap):
    moves = []
    for s in range(1, (pools + 1) // 2):
        moves += [(s, 0, cap), (pools - s, 0, cap)]
    if pools % 2 == 0:
        large = cap - 1
        moves += [(pools // 2, 0, large), (pools // 2, large, cap - large)]
    waits = [None] + [max(0, i - 2) for i in range(1, len(moves))]
    waits[-1] = len(moves) - 2
    return moves, waits


def body(wavefunctions, potentials, pert_order, partners):
    local_k, columns, stacked, bands = wavefunctions.shape
    z_points = stacked // 2
    pools = lax.axis_size("pool")
    groups = lax.axis_size("ga")
    cores = lax.axis_size("pert")
    my_pool = lax.axis_index("pool")
    my_core = lax.axis_index("pert")
    my_group = lax.axis_index("ga")
    cap = max(2, local_k // pools + 1)
    half = columns // cores
    share = bands // groups
    ids = jnp.stack([my_pool, my_core, my_group]).astype(jnp.int32)
    waves = wavefunctions.reshape(local_k * cores, half * stacked, bands)
    swap_cores = [(c, cores - 1 - c) for c in range(cores)]

    plan = make_plan(ids, partners, pools, local_k, cap)
    moves, waits = transfers(pools, cap)
    gives = [pick(plan, ids, waves, pools, cap, move) for move in moves]
    potentials = after(potentials, gives[0])

    per_device = potentials.shape[0]
    by_half = potentials.reshape(per_device, cores, half, stacked)
    mine_now = lax.dynamic_index_in_dim(by_half, my_core, 1, keepdims=False)
    theirs_now = lax.dynamic_index_in_dim(by_half, 1 - my_core, 1, keepdims=False)
    other_pots = lax.ppermute(theirs_now, "pert", swap_cores)
    ordered = jnp.roll(pert_order.reshape(cores, per_device), -my_core, axis=0).reshape(-1)
    stored = jnp.where(
        my_core == 0, jnp.stack([mine_now, other_pots]), jnp.stack([other_pots, mine_now])
    ).reshape((cores * per_device,) + mine_now.shape[1:])
    options = jnp.arange(cores * per_device, dtype=jnp.int32)
    chosen = jnp.sum(
        jnp.where(
            (ordered[:, None] == options[None, :])[:, :, None, None], stored[None],
            jnp.zeros((), F32),
        ),
        axis=1,
    ).reshape(cores * per_device, half, 2, z_points)
    pots = jnp.moveaxis(chosen, 2, 1).reshape(cores * per_device, 2, half * z_points, 1)
    pots = jnp.broadcast_to(pots, pots.shape[:3] + (bands,))
    table = dft_table(z_points)
    scaling = 1.0 / math.sqrt(columns * groups * z_points)

    landed = []

    def send(i, *others):
        shift = moves[i][0]
        others += () if waits[i] is None else (landed[waits[i]],)
        pairs = [(p, (p + shift) % pools) for p in range(pools)]
        landed.append(lax.ppermute(after(gives[i], *others), "pool", pairs))

    for i in range(len(moves) - 1):
        send(i)
    chunks = [((0, 0, cap), waves), *zip(moves, landed), (moves[-1], None)]
    kept, got, terms = [], [], []
    result = None

    def exchange(i):
        sent = []
        size = piece_of(kept[i].shape[0])
        for step in range(1, groups):
            rows = slice(step * share, (step + 1) * share)
            pairs = [(g, (g + step) % groups) for g in range(groups)]
            total = jnp.concatenate(
                [
                    kept[i][at * size : at * size + piece.shape[0], :, rows]
                    + piece[:, :, rows].astype(F32)
                    for at, piece in enumerate(got[i])
                ],
                axis=0,
            )
            sent.append(lax.ppermute(total.astype(BF16), "ga", pairs))
        terms.append(sent)

    finished = 0

    def finish(until, result):
        parcels = [(chunks[i][0], kept[i], got[i], terms[i]) for i in range(finished, until)]
        return combine(plan, result, parcels, local_k, pools, cap, scaling)

    last = len(chunks) - 1
    for i, (chunk, other) in enumerate(chunks):
        if i == last:
            send(i - 1, *([] if result is None else [result]))
            other = landed[-1]
        if i >= 1:
            other = after(other, kept[i - 1])
        if i >= LAG_CORE:
            exchange(i - LAG_CORE)
            other = after(other, *got[i - LAG_CORE])
        if i >= LAG_GROUP:
            other = after(other, *terms[i - LAG_GROUP])
        if last - i in COMBINE and i - LAG_GROUP + 1 > finished:
            result = finish(i - LAG_GROUP + 1, result)
            finished = i - LAG_GROUP + 1
            other = after(other, result)
        if i == 0:
            other = after(other, *gives[1:])
        keep, *gives_now = couple(plan, ids, table, pots, waves, other, chunk, pools, cap, groups)
        kept.append(keep)
        got.append([lax.ppermute(give, "pert", swap_cores) for give in gives_now])
    for i in range(len(terms), len(chunks)):
        exchange(i)
    result = finish(len(chunks), result)
    return result.reshape(local_k, per_device, 2, share, bands)


LAG_CORE, LAG_GROUP = 1, 2
COMBINE = (1,)


def solution(mesh):
    return jax.shard_map(
        body,
        mesh=mesh,
        in_specs=(P("pool", "ga", None, None), P(("pb", "pert"), "ga", None), P(), P("pb")),
        out_specs=P(("pb", "pool"), "pert", None, "ga", None),
        check_vma=False,
    )
```

```python
import functools
import math

import jax
import jax.numpy as jnp
from jax import lax
from jax.experimental import pallas as pl
from jax.experimental.pallas import tpu as pltpu
from jax.sharding import PartitionSpec as P

BF16 = jnp.bfloat16
F32 = jnp.float32
ANY = pl.BlockSpec(memory_space=pl.ANY)
SMEM = pl.BlockSpec(memory_space=pltpu.SMEM)
VMEM_LIMIT = 60 * 1024 * 1024
LIGHT = pl.CostEstimate(flops=1, bytes_accessed=1024, transcendentals=0)
PARAMS = pltpu.CompilerParams(vmem_limit_bytes=VMEM_LIMIT)


def dft_table(length):
    positions = jnp.arange(length, dtype=jnp.int32)
    product = positions[:, None] * positions[None, :] % length
    angles = product.astype(F32) * (2.0 * math.pi / length)
    cosine = jnp.cos(angles) / math.sqrt(length)
    sine_part = jnp.sin(angles) / math.sqrt(length)
    upper_rows = jnp.concatenate([cosine, -sine_part], axis=1)
    bottom = jnp.concatenate([sine_part, cosine], axis=1)
    return jnp.concatenate([upper_rows, bottom], axis=0).astype(BF16)


def plan_kernel(pools, local_k, cap, ids, partners, plan):
    me = ids[0]
    size = pools * cap
    counts = 3 * size

    def clear(i, carry):
        plan[i] = 0
        return carry

    lax.fori_loop(0, counts + pools, clear, 0, unroll=8)

    def visit(t, tally):
        want = partners[me * local_k + t]
        holder = lax.div(want, local_k)
        shift = lax.rem(me - holder + pools, pools)
        slot = plan[counts + shift]
        plan[shift * cap + slot] = t
        plan[size + shift * cap + slot] = want - holder * local_k
        plan[counts + shift] = slot + 1
        after = []
        for shift in range(1, pools):
            taker = lax.rem(me + shift, pools)
            want = partners[taker * local_k + t]
            slot = tally[shift - 1]
            mine = lax.div(want, local_k) == me
            entry = 2 * size + shift * cap + jnp.minimum(slot, cap - 1)
            plan[entry] = jnp.where(mine, lax.rem(want, local_k), plan[entry])
            after.append(slot + mine.astype(jnp.int32))
        return tuple(after)

    lax.fori_loop(0, local_k, visit, (jnp.int32(0),) * (pools - 1), unroll=2)


def make_plan(ids, partners, pools, local_k, cap):
    return pl.pallas_call(
        functools.partial(plan_kernel, pools, local_k, cap),
        out_shape=jax.ShapeDtypeStruct((3 * pools * cap + pools,), jnp.int32),
        in_specs=[SMEM, SMEM],
        out_specs=SMEM,
        cost_estimate=LIGHT,
        name="plan",
    )(ids, partners)


def pick_kernel(base, plan, ids, waves, give, sems):
    copies = [
        pltpu.make_async_copy(waves.at[plan[base + i] * 2 + ids[1]], give.at[i], sems.at[i])
        for i in range(give.shape[0])
    ]
    for copy in copies:
        copy.start()
    for copy in copies:
        copy.wait()


def pick(plan, ids, waves, pools, cap, chunk):
    shift, first, count = chunk
    return pl.pallas_call(
        functools.partial(pick_kernel, (2 * pools + shift) * cap + first),
        out_shape=jax.ShapeDtypeStruct((count,) + waves.shape[1:], waves.dtype),
        in_specs=[SMEM, SMEM, ANY],
        out_specs=pl.BlockSpec(memory_space=pltpu.VMEM),
        scratch_shapes=[pltpu.SemaphoreType.DMA((count,))],
        compiler_params=PARAMS,
        cost_estimate=LIGHT,
        name="pick",
    )(plan, ids, waves)


def to_real(own, other, table, z_points):
    stacked = 2 * z_points
    bands = own.shape[1]
    parts = [[], [], [], []]
    for c in range(own.shape[0] // stacked):
        rows = slice(c * stacked, (c + 1) * stacked)
        pair = jnp.concatenate([own[rows], other[rows]], axis=1)
        out = jnp.dot(table, pair, preferred_element_type=F32)
        parts[0].append(out[:z_points, :bands])
        parts[1].append(out[z_points:, :bands])
        parts[2].append(out[:z_points, bands:])
        parts[3].append(out[z_points:, bands:])
    return [jnp.concatenate(part, axis=0).astype(BF16) for part in parts]


def piece_of(count):
    return max(1, count // 2)


def couple_kernel(shape, plan, ids, table, pots, own, other, keep, *rest):
    number, first, size, groups, z_points = shape
    gives, hold = rest[:-1], rest[-1]

    @pl.when(first + pl.program_id(0) < plan[number])
    def _():
        own_re, own_im, o_re, o_im = to_real(own[0], other[0], table[...], z_points)
        u_re, u_im = own_re.astype(F32), own_im.astype(F32)
        both_o = jnp.concatenate([o_re, o_im], axis=1).T
        bands = o_re.shape[1]
        share = bands // groups
        mine = pots.shape[0] // 2
        starts = [
            pl.multiple_of(lax.rem(g - ids[2] + groups, groups) * share, share)
            for g in range(groups)
        ]
        for j in range(2 * mine):
            p_re, p_im = pots[j, 0], pots[j, 1]
            w_re = (p_re * u_re - p_im * u_im).astype(BF16)
            w_im = (p_re * u_im + p_im * u_re).astype(BF16)
            both = jnp.dot(
                both_o, jnp.concatenate([w_re, w_im], axis=1), preferred_element_type=F32
            )
            real = both[:bands, :bands] + both[bands:, bands:]
            imag = both[:bands, bands:] - both[bands:, :bands]
            for part, value in ((0, real), (1, imag)):
                for g in range(groups):
                    rows = value[g * share : (g + 1) * share]
                    if j < mine:
                        keep[0, 2 * j + part, pl.ds(starts[g], share), :] = rows
                    else:
                        place = 2 * (j - mine) + part
                        hold[place, pl.ds(starts[g], share), :] = rows.astype(BF16)

        for at, give in enumerate(gives):

            @pl.when(pl.program_id(0) // size == at)
            def _(give=give):
                give[0] = hold[...]


def couple(plan, ids, table, pots, waves, other, chunk, pools, cap, groups):
    shift, first, count = chunk
    half, bands = waves.shape[1:]
    parts = pots.shape[0]
    base = shift * cap + first
    block = (1, half, bands)
    own_block = pl.BlockSpec(block, lambda i, plan, ids: (plan[base + i] * 2 + ids[1], 0, 0))
    if shift == 0:
        other_block = pl.BlockSpec(
            block, lambda i, plan, ids: (plan[pools * cap + base + i] * 2 + ids[1], 0, 0)
        )
    else:
        other_block = pl.BlockSpec(block, lambda i, plan, ids: (i, 0, 0))
    out_block = (1, parts, bands, bands)
    size = piece_of(count)
    pieces = [(at, min(size, count - at)) for at in range(0, count, size)]
    shape = (3 * pools * cap + shift, first, size, groups, table.shape[0] // 2)
    return pl.pallas_call(
        functools.partial(couple_kernel, shape),
        grid_spec=pltpu.PrefetchScalarGridSpec(
            num_scalar_prefetch=2,
            grid=(count,),
            in_specs=[
                pl.BlockSpec(table.shape, lambda i, plan, ids: (0, 0)),
                pl.BlockSpec(pots.shape, lambda i, plan, ids: (0, 0, 0, 0)),
                own_block, other_block,
            ],
            out_specs=[pl.BlockSpec(out_block, lambda i, plan, ids: (i, 0, 0, 0))] + [
                pl.BlockSpec(
                    out_block,
                    lambda i, plan, ids, at=at, size=size: (jnp.clip(i - at, 0, size - 1), 0, 0, 0),
                )
                for at, size in pieces
            ],
            scratch_shapes=[pltpu.VMEM((parts, bands, bands), BF16)],
        ),
        out_shape=[jax.ShapeDtypeStruct((count, parts, bands, bands), F32)] + [
            jax.ShapeDtypeStruct((size, parts, bands, bands), BF16) for _, size in pieces
        ],
        compiler_params=PARAMS,
        cost_estimate=LIGHT,
        name="couple",
    )(plan, ids, table, pots, waves, other)


def combine_kernel(shapes, others, scaling, plan, *refs):
    result, stage, sems = refs[-3:]
    terms = list(refs[-3 - sum(1 + shape[4] + others for shape in shapes) : -3])
    blocks = []
    for number, base, first, count, pieces in shapes:
        kept = terms.pop(0)
        added = [([terms.pop(0) for _ in range(pieces)], piece_of(count))]
        added += [([terms.pop(0)], count) for _ in range(others)]
        for i in range(count):
            blocks.append((number, base + i, first + i, kept, added, i))

    def each(action):
        for at, (number, entry, slot, kept, added, i) in enumerate(blocks):

            @pl.when(slot < plan[number])
            def _(at=at, entry=entry, kept=kept, added=added, i=i):
                copy = pltpu.make_async_copy(stage.at[at], result.at[plan[entry]], sems.at[at])
                action(at, copy, kept, added, i)

    def add(at, copy, kept, added, i):
        value = kept[i]
        for pieces, size in added:
            value = value + pieces[i // size][i % size].astype(F32)
        stage[at] = (value * scaling).astype(BF16)
        copy.start()

    each(add)
    each(lambda at, copy, kept, added, i: copy.wait())


def combine(plan, before, parcels, local_k, pools, cap, scaling):
    terms, shapes, total = [], [], 0
    for (shift, first, count), kept, got, arrived in parcels:
        terms += [kept, *got, *arrived]
        shapes.append((3 * pools * cap + shift, shift * cap + first, first, count, len(got)))
        total += count
        others = len(arrived)
        parts, share, bands = arrived[0].shape[1:]
    blocks = [
        pl.BlockSpec((term.shape[0], parts, share, bands), lambda i, plan: (0, 0, 0, 0))
        for term in terms
    ]
    operands = ([] if before is None else [before]) + terms
    return pl.pallas_call(
        functools.partial(combine_kernel, shapes, others, scaling),
        grid_spec=pltpu.PrefetchScalarGridSpec(
            num_scalar_prefetch=1,
            grid=(1,),
            in_specs=([] if before is None else [ANY]) + blocks,
            out_specs=ANY,
            scratch_shapes=[
                pltpu.VMEM((total, parts, share, bands), BF16),
                pltpu.SemaphoreType.DMA((total,)),
            ],
        ),
        out_shape=jax.ShapeDtypeStruct((local_k, parts, share, bands), BF16),
        input_output_aliases={} if before is None else {1: 0},
        compiler_params=PARAMS,
        cost_estimate=LIGHT,
        name="combine",
    )(plan, *operands)


def after(value, *others):
    return lax.optimization_barrier((value, *others))[0]


def transfers(pools, cap):
    moves = []
    for s in range(1, (pools + 1) // 2):
        moves += [(s, 0, cap), (pools - s, 0, cap)]
    if pools % 2 == 0:
        large = (3 * cap + 2) // 5
        moves += [(pools // 2, 0, large), (pools // 2, large, cap - large)]
    waits = [None] + [max(0, i - 2) for i in range(1, len(moves))]
    return moves, waits


def body(wavefunctions, potentials, pert_order, partners):
    local_k, columns, stacked, bands = wavefunctions.shape
    z_points = stacked // 2
    pools = lax.axis_size("pool")
    groups = lax.axis_size("ga")
    cores = lax.axis_size("pert")
    my_pool = lax.axis_index("pool")
    my_core = lax.axis_index("pert")
    my_group = lax.axis_index("ga")
    cap = max(2, local_k // pools + 1)
    half = columns // cores
    share = bands // groups
    ids = jnp.stack([my_pool, my_core, my_group]).astype(jnp.int32)
    waves = wavefunctions.reshape(local_k * cores, half * stacked, bands)
    swap_cores = [(c, cores - 1 - c) for c in range(cores)]

    plan = make_plan(ids, partners, pools, local_k, cap)
    moves, waits = transfers(pools, cap)
    gives = [pick(plan, ids, waves, pools, cap, move) for move in moves]
    potentials = after(potentials, gives[0])

    per_device = potentials.shape[0]
    by_half = potentials.reshape(per_device, cores, half, stacked)
    mine_now = lax.dynamic_index_in_dim(by_half, my_core, 1, keepdims=False)
    theirs_now = lax.dynamic_index_in_dim(by_half, 1 - my_core, 1, keepdims=False)
    other_pots = lax.ppermute(theirs_now, "pert", swap_cores)
    ordered = jnp.roll(pert_order.reshape(cores, per_device), -my_core, axis=0).reshape(-1)
    stored = jnp.where(
        my_core == 0, jnp.stack([mine_now, other_pots]), jnp.stack([other_pots, mine_now])
    ).reshape((cores * per_device,) + mine_now.shape[1:])
    options = jnp.arange(cores * per_device, dtype=jnp.int32)
    chosen = jnp.sum(
        jnp.where(
            (ordered[:, None] == options[None, :])[:, :, None, None], stored[None],
            jnp.zeros((), F32),
        ),
        axis=1,
    ).reshape(cores * per_device, half, 2, z_points)
    pots = jnp.moveaxis(chosen, 2, 1).reshape(cores * per_device, 2, half * z_points, 1)
    pots = jnp.broadcast_to(pots, pots.shape[:3] + (bands,))
    table = dft_table(z_points)
    scaling = 1.0 / math.sqrt(columns * groups * z_points)

    landed = []
    for move, wait, give in zip(moves, waits, gives):
        if wait is not None:
            give = after(give, landed[wait])
        pairs = [(p, (p + move[0]) % pools) for p in range(pools)]
        landed.append(lax.ppermute(give, "pool", pairs))

    chunks = [((0, 0, cap), waves), *zip(moves, landed)]
    kept, got, terms = [], [], []
    result = None

    def exchange(i):
        sent = []
        size = piece_of(kept[i].shape[0])
        for step in range(1, groups):
            rows = slice(step * share, (step + 1) * share)
            pairs = [(g, (g + step) % groups) for g in range(groups)]
            total = jnp.concatenate(
                [
                    kept[i][at * size : at * size + piece.shape[0], :, rows]
                    + piece[:, :, rows].astype(F32)
                    for at, piece in enumerate(got[i])
                ],
                axis=0,
            )
            sent.append(lax.ppermute(total.astype(BF16), "ga", pairs))
        terms.append(sent)

    finished = 0

    def finish(until, result):
        parcels = [(chunks[i][0], kept[i], got[i], terms[i]) for i in range(finished, until)]
        return combine(plan, result, parcels, local_k, pools, cap, scaling)

    last = len(chunks) - 1
    for i, (chunk, other) in enumerate(chunks):
        if i >= 1:
            other = after(other, kept[i - 1])
        if i >= LAG_CORE:
            exchange(i - LAG_CORE)
            other = after(other, *got[i - LAG_CORE])
        if i >= LAG_GROUP:
            other = after(other, *terms[i - LAG_GROUP])
        if last - i in COMBINE and i - LAG_GROUP > finished:
            result = finish(i - LAG_GROUP, result)
            finished = i - LAG_GROUP
            other = after(other, result)
        keep, *gives_now = couple(plan, ids, table, pots, waves, other, chunk, pools, cap, groups)
        kept.append(keep)
        if i >= last - 1:
            gives_now[-1] = after(gives_now[-1], *terms[i - 1])
        if i == last - 1:
            gives_now[-1] = after(gives_now[-1], landed[-1])
        got.append([lax.ppermute(give, "pert", swap_cores) for give in gives_now])
    for i in range(len(terms), len(chunks)):
        exchange(i)
    result = finish(len(chunks), result)
    return result.reshape(local_k, per_device, 2, share, bands)


LAG_CORE, LAG_GROUP = 1, 2
COMBINE = (0,)


def solution(mesh):
    return jax.shard_map(
        body,
        mesh=mesh,
        in_specs=(P("pool", "ga", None, None), P(("pb", "pert"), "ga", None), P(), P("pb")),
        out_specs=P(("pb", "pool"), "pert", None, "ga", None),
        check_vma=False,
    )
```

```python
import functools
import math

import jax
import jax.numpy as jnp
from jax import lax
from jax.experimental import pallas as pl
from jax.experimental.pallas import tpu as pltpu
from jax.sharding import PartitionSpec as P

BF16 = jnp.bfloat16
F32 = jnp.float32
ANY = pl.BlockSpec(memory_space=pl.ANY)
SMEM = pl.BlockSpec(memory_space=pltpu.SMEM)
VMEM_LIMIT = 60 * 1024 * 1024
LIGHT = pl.CostEstimate(flops=1, bytes_accessed=1024, transcendentals=0)
PARAMS = pltpu.CompilerParams(vmem_limit_bytes=VMEM_LIMIT)


def dft_table(length):
    positions = jnp.arange(length, dtype=jnp.int32)
    product = positions[:, None] * positions[None, :] % length
    angles = product.astype(F32) * (2.0 * math.pi / length)
    cosine = jnp.cos(angles) / math.sqrt(length)
    sine_part = jnp.sin(angles) / math.sqrt(length)
    upper_rows = jnp.concatenate([cosine, -sine_part], axis=1)
    bottom = jnp.concatenate([sine_part, cosine], axis=1)
    return jnp.concatenate([upper_rows, bottom], axis=0).astype(BF16)


def plan_kernel(pools, local_k, cap, ids, partners, plan):
    me = ids[0]
    size = pools * cap
    counts = 3 * size

    def clear(i, carry):
        plan[i] = 0
        return carry

    lax.fori_loop(0, counts + pools, clear, 0, unroll=8)

    def visit(t, tally):
        want = partners[me * local_k + t]
        holder = lax.div(want, local_k)
        shift = lax.rem(me - holder + pools, pools)
        slot = plan[counts + shift]
        plan[shift * cap + slot] = t
        plan[size + shift * cap + slot] = want - holder * local_k
        plan[counts + shift] = slot + 1
        after = []
        for shift in range(1, pools):
            taker = lax.rem(me + shift, pools)
            want = partners[taker * local_k + t]
            slot = tally[shift - 1]
            mine = lax.div(want, local_k) == me
            entry = 2 * size + shift * cap + jnp.minimum(slot, cap - 1)
            plan[entry] = jnp.where(mine, lax.rem(want, local_k), plan[entry])
            after.append(slot + mine.astype(jnp.int32))
        return tuple(after)

    lax.fori_loop(0, local_k, visit, (jnp.int32(0),) * (pools - 1), unroll=2)


def make_plan(ids, partners, pools, local_k, cap):
    return pl.pallas_call(
        functools.partial(plan_kernel, pools, local_k, cap),
        out_shape=jax.ShapeDtypeStruct((3 * pools * cap + pools,), jnp.int32),
        in_specs=[SMEM, SMEM],
        out_specs=SMEM,
        cost_estimate=LIGHT,
        name="plan",
    )(ids, partners)


def pick_kernel(base, plan, ids, waves, give, sems):
    copies = [
        pltpu.make_async_copy(waves.at[plan[base + i] * 2 + ids[1]], give.at[i], sems.at[i])
        for i in range(give.shape[0])
    ]
    for copy in copies:
        copy.start()
    for copy in copies:
        copy.wait()


def pick(plan, ids, waves, pools, cap, chunk):
    shift, first, count = chunk
    return pl.pallas_call(
        functools.partial(pick_kernel, (2 * pools + shift) * cap + first),
        out_shape=jax.ShapeDtypeStruct((count,) + waves.shape[1:], waves.dtype),
        in_specs=[SMEM, SMEM, ANY],
        out_specs=pl.BlockSpec(memory_space=pltpu.VMEM),
        scratch_shapes=[pltpu.SemaphoreType.DMA((count,))],
        compiler_params=PARAMS,
        cost_estimate=LIGHT,
        name="pick",
    )(plan, ids, waves)


def to_real(own, other, table, z_points):
    stacked = 2 * z_points
    bands = own.shape[1]
    parts = [[], [], [], []]
    for c in range(own.shape[0] // stacked):
        rows = slice(c * stacked, (c + 1) * stacked)
        pair = jnp.concatenate([own[rows], other[rows]], axis=1)
        out = jnp.dot(table, pair, preferred_element_type=F32)
        parts[0].append(out[:z_points, :bands])
        parts[1].append(out[z_points:, :bands])
        parts[2].append(out[:z_points, bands:])
        parts[3].append(out[z_points:, bands:])
    return [jnp.concatenate(part, axis=0).astype(BF16) for part in parts]


def piece_of(count):
    return max(1, count // 2)


def couple_kernel(shape, plan, ids, table, pots, own, other, keep, *rest):
    number, first, size, groups, z_points = shape
    gives, hold = rest[:-1], rest[-1]

    @pl.when(first + pl.program_id(0) < plan[number])
    def _():
        own_re, own_im, o_re, o_im = to_real(own[0], other[0], table[...], z_points)
        u_re, u_im = own_re.astype(F32), own_im.astype(F32)
        both_o = jnp.concatenate([o_re, o_im], axis=1).T
        bands = o_re.shape[1]
        share = bands // groups
        mine = pots.shape[0] // 2
        starts = [
            pl.multiple_of(lax.rem(g - ids[2] + groups, groups) * share, share)
            for g in range(groups)
        ]
        for j in range(2 * mine):
            p_re, p_im = pots[j, 0], pots[j, 1]
            w_re = (p_re * u_re - p_im * u_im).astype(BF16)
            w_im = (p_re * u_im + p_im * u_re).astype(BF16)
            both = jnp.dot(
                both_o, jnp.concatenate([w_re, w_im], axis=1), preferred_element_type=F32
            )
            real = both[:bands, :bands] + both[bands:, bands:]
            imag = both[:bands, bands:] - both[bands:, :bands]
            for part, value in ((0, real), (1, imag)):
                for g in range(groups):
                    rows = value[g * share : (g + 1) * share]
                    if j < mine:
                        keep[0, 2 * j + part, pl.ds(starts[g], share), :] = rows
                    else:
                        place = 2 * (j - mine) + part
                        hold[place, pl.ds(starts[g], share), :] = rows.astype(BF16)

        for at, give in enumerate(gives):

            @pl.when(pl.program_id(0) // size == at)
            def _(give=give):
                give[0] = hold[...]


def couple(plan, ids, table, pots, waves, other, chunk, pools, cap, groups):
    shift, first, count = chunk
    half, bands = waves.shape[1:]
    parts = pots.shape[0]
    base = shift * cap + first
    block = (1, half, bands)
    own_block = pl.BlockSpec(block, lambda i, plan, ids: (plan[base + i] * 2 + ids[1], 0, 0))
    if shift == 0:
        other_block = pl.BlockSpec(
            block, lambda i, plan, ids: (plan[pools * cap + base + i] * 2 + ids[1], 0, 0)
        )
    else:
        other_block = pl.BlockSpec(block, lambda i, plan, ids: (i, 0, 0))
    out_block = (1, parts, bands, bands)
    size = piece_of(count)
    pieces = [(at, min(size, count - at)) for at in range(0, count, size)]
    shape = (3 * pools * cap + shift, first, size, groups, table.shape[0] // 2)
    return pl.pallas_call(
        functools.partial(couple_kernel, shape),
        grid_spec=pltpu.PrefetchScalarGridSpec(
            num_scalar_prefetch=2,
            grid=(count,),
            in_specs=[
                pl.BlockSpec(table.shape, lambda i, plan, ids: (0, 0)),
                pl.BlockSpec(pots.shape, lambda i, plan, ids: (0, 0, 0, 0)),
                own_block, other_block,
            ],
            out_specs=[pl.BlockSpec(out_block, lambda i, plan, ids: (i, 0, 0, 0))] + [
                pl.BlockSpec(
                    out_block,
                    lambda i, plan, ids, at=at, size=size: (jnp.clip(i - at, 0, size - 1), 0, 0, 0),
                )
                for at, size in pieces
            ],
            scratch_shapes=[pltpu.VMEM((parts, bands, bands), BF16)],
        ),
        out_shape=[jax.ShapeDtypeStruct((count, parts, bands, bands), F32)] + [
            jax.ShapeDtypeStruct((size, parts, bands, bands), BF16) for _, size in pieces
        ],
        compiler_params=PARAMS,
        cost_estimate=LIGHT,
        name="couple",
    )(plan, ids, table, pots, waves, other)


def combine_kernel(shapes, others, scaling, plan, *refs):
    result, stage, sems = refs[-3:]
    terms = list(refs[-3 - sum(1 + shape[4] + others for shape in shapes) : -3])
    blocks = []
    for number, base, first, count, pieces in shapes:
        kept = terms.pop(0)
        added = [([terms.pop(0) for _ in range(pieces)], piece_of(count))]
        added += [([terms.pop(0)], count) for _ in range(others)]
        for i in range(count):
            blocks.append((number, base + i, first + i, kept, added, i))

    def each(action):
        for at, (number, entry, slot, kept, added, i) in enumerate(blocks):

            @pl.when(slot < plan[number])
            def _(at=at, entry=entry, kept=kept, added=added, i=i):
                copy = pltpu.make_async_copy(stage.at[at], result.at[plan[entry]], sems.at[at])
                action(at, copy, kept, added, i)

    def add(at, copy, kept, added, i):
        value = kept[i]
        for pieces, size in added:
            value = value + pieces[i // size][i % size].astype(F32)
        stage[at] = (value * scaling).astype(BF16)
        copy.start()

    each(add)
    each(lambda at, copy, kept, added, i: copy.wait())


def combine(plan, before, parcels, local_k, pools, cap, scaling):
    terms, shapes, total = [], [], 0
    for (shift, first, count), kept, got, arrived in parcels:
        terms += [kept, *got, *arrived]
        shapes.append((3 * pools * cap + shift, shift * cap + first, first, count, len(got)))
        total += count
        others = len(arrived)
        parts, share, bands = arrived[0].shape[1:]
    blocks = [
        pl.BlockSpec((term.shape[0], parts, share, bands), lambda i, plan: (0, 0, 0, 0))
        for term in terms
    ]
    operands = ([] if before is None else [before]) + terms
    return pl.pallas_call(
        functools.partial(combine_kernel, shapes, others, scaling),
        grid_spec=pltpu.PrefetchScalarGridSpec(
            num_scalar_prefetch=1,
            grid=(1,),
            in_specs=([] if before is None else [ANY]) + blocks,
            out_specs=ANY,
            scratch_shapes=[
                pltpu.VMEM((total, parts, share, bands), BF16),
                pltpu.SemaphoreType.DMA((total,)),
            ],
        ),
        out_shape=jax.ShapeDtypeStruct((local_k, parts, share, bands), BF16),
        input_output_aliases={} if before is None else {1: 0},
        compiler_params=PARAMS,
        cost_estimate=LIGHT,
        name="combine",
    )(plan, *operands)


def after(value, *others):
    return lax.optimization_barrier((value, *others))[0]


def transfers(pools, cap):
    moves = []
    for s in range(1, (pools + 1) // 2):
        moves += [(s, 0, cap), (pools - s, 0, cap)]
    if pools % 2 == 0:
        large = (3 * cap + 2) // 5
        moves += [(pools // 2, 0, large), (pools // 2, large, cap - large)]
    waits = [None] + [max(0, i - 2) for i in range(1, len(moves))]
    return moves, waits


def body(wavefunctions, potentials, pert_order, partners):
    local_k, columns, stacked, bands = wavefunctions.shape
    z_points = stacked // 2
    pools = lax.axis_size("pool")
    groups = lax.axis_size("ga")
    cores = lax.axis_size("pert")
    my_pool = lax.axis_index("pool")
    my_core = lax.axis_index("pert")
    my_group = lax.axis_index("ga")
    cap = max(2, local_k // pools + 1)
    half = columns // cores
    share = bands // groups
    ids = jnp.stack([my_pool, my_core, my_group]).astype(jnp.int32)
    waves = wavefunctions.reshape(local_k * cores, half * stacked, bands)
    swap_cores = [(c, cores - 1 - c) for c in range(cores)]

    plan = make_plan(ids, partners, pools, local_k, cap)
    moves, waits = transfers(pools, cap)
    gives = [pick(plan, ids, waves, pools, cap, move) for move in moves]
    potentials = after(potentials, gives[0])

    per_device = potentials.shape[0]
    by_half = potentials.reshape(per_device, cores, half, stacked)
    mine_now = lax.dynamic_index_in_dim(by_half, my_core, 1, keepdims=False)
    theirs_now = lax.dynamic_index_in_dim(by_half, 1 - my_core, 1, keepdims=False)
    other_pots = lax.ppermute(theirs_now, "pert", swap_cores)
    ordered = jnp.roll(pert_order.reshape(cores, per_device), -my_core, axis=0).reshape(-1)
    stored = jnp.where(
        my_core == 0, jnp.stack([mine_now, other_pots]), jnp.stack([other_pots, mine_now])
    ).reshape((cores * per_device,) + mine_now.shape[1:])
    options = jnp.arange(cores * per_device, dtype=jnp.int32)
    chosen = jnp.sum(
        jnp.where(
            (ordered[:, None] == options[None, :])[:, :, None, None], stored[None],
            jnp.zeros((), F32),
        ),
        axis=1,
    ).reshape(cores * per_device, half, 2, z_points)
    pots = jnp.moveaxis(chosen, 2, 1).reshape(cores * per_device, 2, half * z_points, 1)
    pots = jnp.broadcast_to(pots, pots.shape[:3] + (bands,))
    table = dft_table(z_points)
    scaling = 1.0 / math.sqrt(columns * groups * z_points)

    landed = []
    for move, wait, give in zip(moves, waits, gives):
        if wait is not None:
            give = after(give, landed[wait])
        pairs = [(p, (p + move[0]) % pools) for p in range(pools)]
        landed.append(lax.ppermute(give, "pool", pairs))

    chunks = [((0, 0, cap), waves), *zip(moves, landed)]
    kept, got, terms = [], [], []
    result = None

    def exchange(i):
        sent = []
        size = piece_of(kept[i].shape[0])
        for step in range(1, groups):
            rows = slice(step * share, (step + 1) * share)
            pairs = [(g, (g + step) % groups) for g in range(groups)]
            total = jnp.concatenate(
                [
                    kept[i][at * size : at * size + piece.shape[0], :, rows]
                    + piece[:, :, rows].astype(F32)
                    for at, piece in enumerate(got[i])
                ],
                axis=0,
            )
            sent.append(lax.ppermute(total.astype(BF16), "ga", pairs))
        terms.append(sent)

    finished = 0

    def finish(until, result):
        parcels = [(chunks[i][0], kept[i], got[i], terms[i]) for i in range(finished, until)]
        return combine(plan, result, parcels, local_k, pools, cap, scaling)

    last = len(chunks) - 1
    for i, (chunk, other) in enumerate(chunks):
        if i >= 1:
            other = after(other, kept[i - 1])
        if i >= LAG_CORE:
            exchange(i - LAG_CORE)
            other = after(other, *got[i - LAG_CORE])
        if i >= LAG_GROUP:
            other = after(other, *terms[i - LAG_GROUP])
        if last - i in COMBINE and i - LAG_GROUP + 1 > finished:
            result = finish(i - LAG_GROUP + 1, result)
            finished = i - LAG_GROUP + 1
            other = after(other, result)
        keep, *gives_now = couple(plan, ids, table, pots, waves, other, chunk, pools, cap, groups)
        kept.append(keep)
        if i >= last - 1:
            gives_now[-1] = after(gives_now[-1], *terms[i - 1])
        if i == last - 1:
            gives_now[-1] = after(gives_now[-1], landed[-1])
        got.append([lax.ppermute(give, "pert", swap_cores) for give in gives_now])
    for i in range(len(terms), len(chunks)):
        exchange(i)
    result = finish(len(chunks), result)
    return result.reshape(local_k, per_device, 2, share, bands)


LAG_CORE, LAG_GROUP = 1, 2
COMBINE = (1,)


def solution(mesh):
    return jax.shard_map(
        body,
        mesh=mesh,
        in_specs=(P("pool", "ga", None, None), P(("pb", "pert"), "ga", None), P(), P("pb")),
        out_specs=P(("pb", "pool"), "pert", None, "ga", None),
        check_vma=False,
    )
```

```python
import functools
import math

import jax
import jax.numpy as jnp
from jax import lax
from jax.experimental import pallas as pl
from jax.experimental.pallas import tpu as pltpu
from jax.sharding import PartitionSpec as P

BF16 = jnp.bfloat16
F32 = jnp.float32
ANY = pl.BlockSpec(memory_space=pl.ANY)
SMEM = pl.BlockSpec(memory_space=pltpu.SMEM)
VMEM_LIMIT = 60 * 1024 * 1024
LIGHT = pl.CostEstimate(flops=1, bytes_accessed=1024, transcendentals=0)
PARAMS = pltpu.CompilerParams(vmem_limit_bytes=VMEM_LIMIT)


def dft_table(length):
    positions = jnp.arange(length, dtype=jnp.int32)
    product = positions[:, None] * positions[None, :] % length
    angles = product.astype(F32) * (2.0 * math.pi / length)
    cosine = jnp.cos(angles) / math.sqrt(length)
    sine_part = jnp.sin(angles) / math.sqrt(length)
    upper_rows = jnp.concatenate([cosine, -sine_part], axis=1)
    bottom = jnp.concatenate([sine_part, cosine], axis=1)
    return jnp.concatenate([upper_rows, bottom], axis=0).astype(BF16)


def plan_kernel(pools, local_k, cap, ids, partners, plan):
    me = ids[0]
    size = pools * cap
    counts = 3 * size

    def clear(i, carry):
        plan[i] = 0
        return carry

    lax.fori_loop(0, counts + pools, clear, 0, unroll=8)

    def visit(t, tally):
        want = partners[me * local_k + t]
        holder = lax.div(want, local_k)
        shift = lax.rem(me - holder + pools, pools)
        slot = plan[counts + shift]
        plan[shift * cap + slot] = t
        plan[size + shift * cap + slot] = want - holder * local_k
        plan[counts + shift] = slot + 1
        after = []
        for shift in range(1, pools):
            taker = lax.rem(me + shift, pools)
            want = partners[taker * local_k + t]
            slot = tally[shift - 1]
            mine = lax.div(want, local_k) == me
            entry = 2 * size + shift * cap + jnp.minimum(slot, cap - 1)
            plan[entry] = jnp.where(mine, lax.rem(want, local_k), plan[entry])
            after.append(slot + mine.astype(jnp.int32))
        return tuple(after)

    lax.fori_loop(0, local_k, visit, (jnp.int32(0),) * (pools - 1), unroll=2)


def make_plan(ids, partners, pools, local_k, cap):
    return pl.pallas_call(
        functools.partial(plan_kernel, pools, local_k, cap),
        out_shape=jax.ShapeDtypeStruct((3 * pools * cap + pools,), jnp.int32),
        in_specs=[SMEM, SMEM],
        out_specs=SMEM,
        cost_estimate=LIGHT,
        name="plan",
    )(ids, partners)


def pick_kernel(base, plan, ids, waves, give, sems):
    copies = [
        pltpu.make_async_copy(waves.at[plan[base + i] * 2 + ids[1]], give.at[i], sems.at[i])
        for i in range(give.shape[0])
    ]
    for copy in copies:
        copy.start()
    for copy in copies:
        copy.wait()


def pick(plan, ids, waves, pools, cap, chunk):
    shift, first, count = chunk
    return pl.pallas_call(
        functools.partial(pick_kernel, (2 * pools + shift) * cap + first),
        out_shape=jax.ShapeDtypeStruct((count,) + waves.shape[1:], waves.dtype),
        in_specs=[SMEM, SMEM, ANY],
        out_specs=pl.BlockSpec(memory_space=pltpu.VMEM),
        scratch_shapes=[pltpu.SemaphoreType.DMA((count,))],
        compiler_params=PARAMS,
        cost_estimate=LIGHT,
        name="pick",
    )(plan, ids, waves)


def to_real(own, other, table, z_points):
    stacked = 2 * z_points
    bands = own.shape[1]
    parts = [[], [], [], []]
    for c in range(own.shape[0] // stacked):
        rows = slice(c * stacked, (c + 1) * stacked)
        pair = jnp.concatenate([own[rows], other[rows]], axis=1)
        out = jnp.dot(table, pair, preferred_element_type=F32)
        parts[0].append(out[:z_points, :bands])
        parts[1].append(out[z_points:, :bands])
        parts[2].append(out[:z_points, bands:])
        parts[3].append(out[z_points:, bands:])
    return [jnp.concatenate(part, axis=0).astype(BF16) for part in parts]


def piece_of(count):
    return max(1, count // 2)


def couple_kernel(shape, plan, ids, table, pots, own, other, keep, *rest):
    number, first, size, groups, z_points = shape
    gives, hold = rest[:-1], rest[-1]

    @pl.when(first + pl.program_id(0) < plan[number])
    def _():
        own_re, own_im, o_re, o_im = to_real(own[0], other[0], table[...], z_points)
        u_re, u_im = own_re.astype(F32), own_im.astype(F32)
        both_o = jnp.concatenate([o_re, o_im], axis=1).T
        bands = o_re.shape[1]
        share = bands // groups
        mine = pots.shape[0] // 2
        starts = [
            pl.multiple_of(lax.rem(g - ids[2] + groups, groups) * share, share)
            for g in range(groups)
        ]
        for j in range(2 * mine):
            p_re, p_im = pots[j, 0], pots[j, 1]
            w_re = (p_re * u_re - p_im * u_im).astype(BF16)
            w_im = (p_re * u_im + p_im * u_re).astype(BF16)
            both = jnp.dot(
                both_o, jnp.concatenate([w_re, w_im], axis=1), preferred_element_type=F32
            )
            real = both[:bands, :bands] + both[bands:, bands:]
            imag = both[:bands, bands:] - both[bands:, :bands]
            for part, value in ((0, real), (1, imag)):
                for g in range(groups):
                    rows = value[g * share : (g + 1) * share]
                    if j < mine:
                        keep[0, 2 * j + part, pl.ds(starts[g], share), :] = rows
                    else:
                        place = 2 * (j - mine) + part
                        hold[place, pl.ds(starts[g], share), :] = rows.astype(BF16)

        for at, give in enumerate(gives):

            @pl.when(pl.program_id(0) // size == at)
            def _(give=give):
                give[0] = hold[...]


def couple(plan, ids, table, pots, waves, other, chunk, pools, cap, groups):
    shift, first, count = chunk
    half, bands = waves.shape[1:]
    parts = pots.shape[0]
    base = shift * cap + first
    block = (1, half, bands)
    own_block = pl.BlockSpec(block, lambda i, plan, ids: (plan[base + i] * 2 + ids[1], 0, 0))
    if shift == 0:
        other_block = pl.BlockSpec(
            block, lambda i, plan, ids: (plan[pools * cap + base + i] * 2 + ids[1], 0, 0)
        )
    else:
        other_block = pl.BlockSpec(block, lambda i, plan, ids: (i, 0, 0))
    out_block = (1, parts, bands, bands)
    size = piece_of(count)
    pieces = [(at, min(size, count - at)) for at in range(0, count, size)]
    shape = (3 * pools * cap + shift, first, size, groups, table.shape[0] // 2)
    return pl.pallas_call(
        functools.partial(couple_kernel, shape),
        grid_spec=pltpu.PrefetchScalarGridSpec(
            num_scalar_prefetch=2,
            grid=(count,),
            in_specs=[
                pl.BlockSpec(table.shape, lambda i, plan, ids: (0, 0)),
                pl.BlockSpec(pots.shape, lambda i, plan, ids: (0, 0, 0, 0)),
                own_block, other_block,
            ],
            out_specs=[pl.BlockSpec(out_block, lambda i, plan, ids: (i, 0, 0, 0))] + [
                pl.BlockSpec(
                    out_block,
                    lambda i, plan, ids, at=at, size=size: (jnp.clip(i - at, 0, size - 1), 0, 0, 0),
                )
                for at, size in pieces
            ],
            scratch_shapes=[pltpu.VMEM((parts, bands, bands), BF16)],
        ),
        out_shape=[jax.ShapeDtypeStruct((count, parts, bands, bands), F32)] + [
            jax.ShapeDtypeStruct((size, parts, bands, bands), BF16) for _, size in pieces
        ],
        compiler_params=PARAMS,
        cost_estimate=LIGHT,
        name="couple",
    )(plan, ids, table, pots, waves, other)


def combine_kernel(shapes, others, scaling, plan, *refs):
    result, stage, sems = refs[-3:]
    terms = list(refs[-3 - sum(1 + shape[4] + others for shape in shapes) : -3])
    blocks = []
    for number, base, first, count, pieces in shapes:
        kept = terms.pop(0)
        added = [([terms.pop(0) for _ in range(pieces)], piece_of(count))]
        added += [([terms.pop(0)], count) for _ in range(others)]
        for i in range(count):
            blocks.append((number, base + i, first + i, kept, added, i))

    def each(action):
        for at, (number, entry, slot, kept, added, i) in enumerate(blocks):

            @pl.when(slot < plan[number])
            def _(at=at, entry=entry, kept=kept, added=added, i=i):
                copy = pltpu.make_async_copy(stage.at[at], result.at[plan[entry]], sems.at[at])
                action(at, copy, kept, added, i)

    def add(at, copy, kept, added, i):
        value = kept[i]
        for pieces, size in added:
            value = value + pieces[i // size][i % size].astype(F32)
        stage[at] = (value * scaling).astype(BF16)
        copy.start()

    each(add)
    each(lambda at, copy, kept, added, i: copy.wait())


def combine(plan, before, parcels, local_k, pools, cap, scaling):
    terms, shapes, total = [], [], 0
    for (shift, first, count), kept, got, arrived in parcels:
        terms += [kept, *got, *arrived]
        shapes.append((3 * pools * cap + shift, shift * cap + first, first, count, len(got)))
        total += count
        others = len(arrived)
        parts, share, bands = arrived[0].shape[1:]
    blocks = [
        pl.BlockSpec((term.shape[0], parts, share, bands), lambda i, plan: (0, 0, 0, 0))
        for term in terms
    ]
    operands = ([] if before is None else [before]) + terms
    return pl.pallas_call(
        functools.partial(combine_kernel, shapes, others, scaling),
        grid_spec=pltpu.PrefetchScalarGridSpec(
            num_scalar_prefetch=1,
            grid=(1,),
            in_specs=([] if before is None else [ANY]) + blocks,
            out_specs=ANY,
            scratch_shapes=[
                pltpu.VMEM((total, parts, share, bands), BF16),
                pltpu.SemaphoreType.DMA((total,)),
            ],
        ),
        out_shape=jax.ShapeDtypeStruct((local_k, parts, share, bands), BF16),
        input_output_aliases={} if before is None else {1: 0},
        compiler_params=PARAMS,
        cost_estimate=LIGHT,
        name="combine",
    )(plan, *operands)


def after(value, *others):
    return lax.optimization_barrier((value, *others))[0]


def transfers(pools, cap):
    moves = []
    for s in range(1, (pools + 1) // 2):
        moves += [(s, 0, cap), (pools - s, 0, cap)]
    if pools % 2 == 0:
        large = (3 * cap + 2) // 5
        moves += [(pools // 2, 0, large), (pools // 2, large, cap - large)]
    waits = [None] + [max(0, i - 2) for i in range(1, len(moves))]
    return moves, waits


def body(wavefunctions, potentials, pert_order, partners):
    local_k, columns, stacked, bands = wavefunctions.shape
    z_points = stacked // 2
    pools = lax.axis_size("pool")
    groups = lax.axis_size("ga")
    cores = lax.axis_size("pert")
    my_pool = lax.axis_index("pool")
    my_core = lax.axis_index("pert")
    my_group = lax.axis_index("ga")
    cap = max(2, local_k // pools + 1)
    half = columns // cores
    share = bands // groups
    ids = jnp.stack([my_pool, my_core, my_group]).astype(jnp.int32)
    waves = wavefunctions.reshape(local_k * cores, half * stacked, bands)
    swap_cores = [(c, cores - 1 - c) for c in range(cores)]

    plan = make_plan(ids, partners, pools, local_k, cap)
    moves, waits = transfers(pools, cap)
    gives = [pick(plan, ids, waves, pools, cap, move) for move in moves]
    potentials = after(potentials, gives[0])

    per_device = potentials.shape[0]
    by_half = potentials.reshape(per_device, cores, half, stacked)
    mine_now = lax.dynamic_index_in_dim(by_half, my_core, 1, keepdims=False)
    theirs_now = lax.dynamic_index_in_dim(by_half, 1 - my_core, 1, keepdims=False)
    other_pots = lax.ppermute(theirs_now, "pert", swap_cores)
    ordered = jnp.roll(pert_order.reshape(cores, per_device), -my_core, axis=0).reshape(-1)
    stored = jnp.where(
        my_core == 0, jnp.stack([mine_now, other_pots]), jnp.stack([other_pots, mine_now])
    ).reshape((cores * per_device,) + mine_now.shape[1:])
    options = jnp.arange(cores * per_device, dtype=jnp.int32)
    chosen = jnp.sum(
        jnp.where(
            (ordered[:, None] == options[None, :])[:, :, None, None], stored[None],
            jnp.zeros((), F32),
        ),
        axis=1,
    ).reshape(cores * per_device, half, 2, z_points)
    pots = jnp.moveaxis(chosen, 2, 1).reshape(cores * per_device, 2, half * z_points, 1)
    pots = jnp.broadcast_to(pots, pots.shape[:3] + (bands,))
    table = dft_table(z_points)
    scaling = 1.0 / math.sqrt(columns * groups * z_points)

    landed = []
    for move, wait, give in zip(moves, waits, gives):
        if wait is not None:
            give = after(give, landed[wait])
        pairs = [(p, (p + move[0]) % pools) for p in range(pools)]
        landed.append(lax.ppermute(give, "pool", pairs))

    chunks = [((0, 0, cap), waves), *zip(moves, landed)]
    kept, got, terms = [], [], []
    result = None

    def exchange(i):
        sent = []
        size = piece_of(kept[i].shape[0])
        for step in range(1, groups):
            rows = slice(step * share, (step + 1) * share)
            pairs = [(g, (g + step) % groups) for g in range(groups)]
            total = jnp.concatenate(
                [
                    kept[i][at * size : at * size + piece.shape[0], :, rows]
                    + piece[:, :, rows].astype(F32)
                    for at, piece in enumerate(got[i])
                ],
                axis=0,
            )
            sent.append(lax.ppermute(total.astype(BF16), "ga", pairs))
        terms.append(sent)

    finished = 0

    def finish(until, result):
        parcels = [(chunks[i][0], kept[i], got[i], terms[i]) for i in range(finished, until)]
        return combine(plan, result, parcels, local_k, pools, cap, scaling)

    last = len(chunks) - 1
    for i, (chunk, other) in enumerate(chunks):
        if i >= 1:
            other = after(other, kept[i - 1])
        if i >= LAG_CORE:
            exchange(i - LAG_CORE)
            other = after(other, *got[i - LAG_CORE])
        if i >= LAG_GROUP:
            other = after(other, *terms[i - LAG_GROUP])
        if last - i in COMBINE and i - LAG_GROUP + 1 > finished:
            result = finish(i - LAG_GROUP + 1, result)
            finished = i - LAG_GROUP + 1
            other = after(other, result)
        keep, *gives_now = couple(plan, ids, table, pots, waves, other, chunk, pools, cap, groups)
        kept.append(keep)
        if i >= last - 1:
            gives_now[-1] = after(gives_now[-1], *terms[i - 1])
        if i == last - 1:
            gives_now[-1] = after(gives_now[-1], landed[-1])
        got.append([lax.ppermute(give, "pert", swap_cores) for give in gives_now])
    for i in range(len(terms), len(chunks)):
        exchange(i)
    result = finish(last, result)
    finished = last
    result = finish(len(chunks), result)
    return result.reshape(local_k, per_device, 2, share, bands)


LAG_CORE, LAG_GROUP = 1, 2
COMBINE = (1,)


def solution(mesh):
    return jax.shard_map(
        body,
        mesh=mesh,
        in_specs=(P("pool", "ga", None, None), P(("pb", "pert"), "ga", None), P(), P("pb")),
        out_specs=P(("pb", "pool"), "pert", None, "ga", None),
        check_vma=False,
    )
```

```python
import functools
import math

import jax
import jax.numpy as jnp
from jax import lax
from jax.experimental import pallas as pl
from jax.experimental.pallas import tpu as pltpu
from jax.sharding import PartitionSpec as P

BF16 = jnp.bfloat16
F32 = jnp.float32
ANY = pl.BlockSpec(memory_space=pl.ANY)
SMEM = pl.BlockSpec(memory_space=pltpu.SMEM)
VMEM_LIMIT = 60 * 1024 * 1024
LIGHT = pl.CostEstimate(flops=1, bytes_accessed=1024, transcendentals=0)
PARAMS = pltpu.CompilerParams(vmem_limit_bytes=VMEM_LIMIT)


def dft_table(length):
    positions = jnp.arange(length, dtype=jnp.int32)
    product = positions[:, None] * positions[None, :] % length
    angles = product.astype(F32) * (2.0 * math.pi / length)
    cosine = jnp.cos(angles) / math.sqrt(length)
    sine_part = jnp.sin(angles) / math.sqrt(length)
    upper_rows = jnp.concatenate([cosine, -sine_part], axis=1)
    bottom = jnp.concatenate([sine_part, cosine], axis=1)
    return jnp.concatenate([upper_rows, bottom], axis=0).astype(BF16)


def plan_kernel(pools, local_k, cap, ids, partners, plan):
    me = ids[0]
    size = pools * cap
    counts = 3 * size

    def clear(i, carry):
        plan[i] = 0
        return carry

    lax.fori_loop(0, counts + pools, clear, 0, unroll=8)

    def visit(t, tally):
        want = partners[me * local_k + t]
        holder = lax.div(want, local_k)
        shift = lax.rem(me - holder + pools, pools)
        slot = plan[counts + shift]
        plan[shift * cap + slot] = t
        plan[size + shift * cap + slot] = want - holder * local_k
        plan[counts + shift] = slot + 1
        after = []
        for shift in range(1, pools):
            taker = lax.rem(me + shift, pools)
            want = partners[taker * local_k + t]
            slot = tally[shift - 1]
            mine = lax.div(want, local_k) == me
            entry = 2 * size + shift * cap + jnp.minimum(slot, cap - 1)
            plan[entry] = jnp.where(mine, lax.rem(want, local_k), plan[entry])
            after.append(slot + mine.astype(jnp.int32))
        return tuple(after)

    lax.fori_loop(0, local_k, visit, (jnp.int32(0),) * (pools - 1), unroll=2)


def make_plan(ids, partners, pools, local_k, cap):
    return pl.pallas_call(
        functools.partial(plan_kernel, pools, local_k, cap),
        out_shape=jax.ShapeDtypeStruct((3 * pools * cap + pools,), jnp.int32),
        in_specs=[SMEM, SMEM],
        out_specs=SMEM,
        cost_estimate=LIGHT,
        name="plan",
    )(ids, partners)


def pick_kernel(base, plan, ids, waves, give, sems):
    copies = [
        pltpu.make_async_copy(waves.at[plan[base + i] * 2 + ids[1]], give.at[i], sems.at[i])
        for i in range(give.shape[0])
    ]
    for copy in copies:
        copy.start()
    for copy in copies:
        copy.wait()


def pick(plan, ids, waves, pools, cap, chunk):
    shift, first, count = chunk
    return pl.pallas_call(
        functools.partial(pick_kernel, (2 * pools + shift) * cap + first),
        out_shape=jax.ShapeDtypeStruct((count,) + waves.shape[1:], waves.dtype),
        in_specs=[SMEM, SMEM, ANY],
        out_specs=pl.BlockSpec(memory_space=pltpu.VMEM),
        scratch_shapes=[pltpu.SemaphoreType.DMA((count,))],
        compiler_params=PARAMS,
        cost_estimate=LIGHT,
        name="pick",
    )(plan, ids, waves)


def to_real(own, other, table, z_points):
    stacked = 2 * z_points
    bands = own.shape[1]
    parts = [[], [], [], []]
    for c in range(own.shape[0] // stacked):
        rows = slice(c * stacked, (c + 1) * stacked)
        pair = jnp.concatenate([own[rows], other[rows]], axis=1)
        out = jnp.dot(table, pair, preferred_element_type=F32)
        parts[0].append(out[:z_points, :bands])
        parts[1].append(out[z_points:, :bands])
        parts[2].append(out[:z_points, bands:])
        parts[3].append(out[z_points:, bands:])
    return [jnp.concatenate(part, axis=0).astype(BF16) for part in parts]


def piece_of(count):
    return max(1, count // 2)


def couple_kernel(shape, plan, ids, table, pots, own, other, keep, *rest):
    number, first, size, groups, z_points = shape
    gives, hold = rest[:-1], rest[-1]

    @pl.when(first + pl.program_id(0) < plan[number])
    def _():
        own_re, own_im, o_re, o_im = to_real(own[0], other[0], table[...], z_points)
        u_re, u_im = own_re.astype(F32), own_im.astype(F32)
        both_o = jnp.concatenate([o_re, o_im], axis=1).T
        bands = o_re.shape[1]
        share = bands // groups
        mine = pots.shape[0] // 2
        starts = [
            pl.multiple_of(lax.rem(g - ids[2] + groups, groups) * share, share)
            for g in range(groups)
        ]
        for j in range(2 * mine):
            p_re, p_im = pots[j, 0], pots[j, 1]
            w_re = (p_re * u_re - p_im * u_im).astype(BF16)
            w_im = (p_re * u_im + p_im * u_re).astype(BF16)
            both = jnp.dot(
                both_o, jnp.concatenate([w_re, w_im], axis=1), preferred_element_type=F32
            )
            real = both[:bands, :bands] + both[bands:, bands:]
            imag = both[:bands, bands:] - both[bands:, :bands]
            for part, value in ((0, real), (1, imag)):
                for g in range(groups):
                    rows = value[g * share : (g + 1) * share]
                    if j < mine:
                        keep[0, 2 * j + part, pl.ds(starts[g], share), :] = rows
                    else:
                        place = 2 * (j - mine) + part
                        hold[place, pl.ds(starts[g], share), :] = rows.astype(BF16)

        for at, give in enumerate(gives):

            @pl.when(pl.program_id(0) // size == at)
            def _(give=give):
                give[0] = hold[...]


def couple(plan, ids, table, pots, waves, other, chunk, pools, cap, groups):
    shift, first, count = chunk
    half, bands = waves.shape[1:]
    parts = pots.shape[0]
    base = shift * cap + first
    block = (1, half, bands)
    own_block = pl.BlockSpec(block, lambda i, plan, ids: (plan[base + i] * 2 + ids[1], 0, 0))
    if shift == 0:
        other_block = pl.BlockSpec(
            block, lambda i, plan, ids: (plan[pools * cap + base + i] * 2 + ids[1], 0, 0)
        )
    else:
        other_block = pl.BlockSpec(block, lambda i, plan, ids: (i, 0, 0))
    out_block = (1, parts, bands, bands)
    size = piece_of(count)
    pieces = [(at, min(size, count - at)) for at in range(0, count, size)]
    shape = (3 * pools * cap + shift, first, size, groups, table.shape[0] // 2)
    return pl.pallas_call(
        functools.partial(couple_kernel, shape),
        grid_spec=pltpu.PrefetchScalarGridSpec(
            num_scalar_prefetch=2,
            grid=(count,),
            in_specs=[
                pl.BlockSpec(table.shape, lambda i, plan, ids: (0, 0)),
                pl.BlockSpec(pots.shape, lambda i, plan, ids: (0, 0, 0, 0)),
                own_block, other_block,
            ],
            out_specs=[pl.BlockSpec(out_block, lambda i, plan, ids: (i, 0, 0, 0))] + [
                pl.BlockSpec(
                    out_block,
                    lambda i, plan, ids, at=at, size=size: (jnp.clip(i - at, 0, size - 1), 0, 0, 0),
                )
                for at, size in pieces
            ],
            scratch_shapes=[pltpu.VMEM((parts, bands, bands), BF16)],
        ),
        out_shape=[jax.ShapeDtypeStruct((count, parts, bands, bands), F32)] + [
            jax.ShapeDtypeStruct((size, parts, bands, bands), BF16) for _, size in pieces
        ],
        compiler_params=PARAMS,
        cost_estimate=LIGHT,
        name="couple",
    )(plan, ids, table, pots, waves, other)


def combine_kernel(shapes, others, scaling, plan, *refs):
    result, stage, sems = refs[-3:]
    terms = list(refs[-3 - sum(1 + shape[4] + others for shape in shapes) : -3])
    blocks = []
    for number, base, first, count, pieces in shapes:
        kept = terms.pop(0)
        added = [([terms.pop(0) for _ in range(pieces)], piece_of(count))]
        added += [([terms.pop(0)], count) for _ in range(others)]
        for i in range(count):
            blocks.append((number, base + i, first + i, kept, added, i))

    def each(action):
        for at, (number, entry, slot, kept, added, i) in enumerate(blocks):

            @pl.when(slot < plan[number])
            def _(at=at, entry=entry, kept=kept, added=added, i=i):
                copy = pltpu.make_async_copy(stage.at[at], result.at[plan[entry]], sems.at[at])
                action(at, copy, kept, added, i)

    def add(at, copy, kept, added, i):
        value = kept[i]
        for pieces, size in added:
            value = value + pieces[i // size][i % size].astype(F32)
        stage[at] = (value * scaling).astype(BF16)
        copy.start()

    each(add)
    each(lambda at, copy, kept, added, i: copy.wait())


def combine(plan, before, parcels, local_k, pools, cap, scaling):
    terms, shapes, total = [], [], 0
    for (shift, first, count), kept, got, arrived in parcels:
        terms += [kept, *got, *arrived]
        shapes.append((3 * pools * cap + shift, shift * cap + first, first, count, len(got)))
        total += count
        others = len(arrived)
        parts, share, bands = arrived[0].shape[1:]
    blocks = [
        pl.BlockSpec((term.shape[0], parts, share, bands), lambda i, plan: (0, 0, 0, 0))
        for term in terms
    ]
    operands = ([] if before is None else [before]) + terms
    return pl.pallas_call(
        functools.partial(combine_kernel, shapes, others, scaling),
        grid_spec=pltpu.PrefetchScalarGridSpec(
            num_scalar_prefetch=1,
            grid=(1,),
            in_specs=([] if before is None else [ANY]) + blocks,
            out_specs=ANY,
            scratch_shapes=[
                pltpu.VMEM((total, parts, share, bands), BF16),
                pltpu.SemaphoreType.DMA((total,)),
            ],
        ),
        out_shape=jax.ShapeDtypeStruct((local_k, parts, share, bands), BF16),
        input_output_aliases={} if before is None else {1: 0},
        compiler_params=PARAMS,
        cost_estimate=LIGHT,
        name="combine",
    )(plan, *operands)


def after(value, *others):
    return lax.optimization_barrier((value, *others))[0]


def transfers(pools, cap):
    moves = []
    for s in range(1, (pools + 1) // 2):
        moves += [(s, 0, cap), (pools - s, 0, cap)]
    if pools % 2 == 0:
        large = (3 * cap + 2) // 5
        moves += [(pools // 2, 0, large), (pools // 2, large, cap - large)]
    waits = [None] + [max(0, i - 2) for i in range(1, len(moves))]
    return moves, waits


def body(wavefunctions, potentials, pert_order, partners):
    local_k, columns, stacked, bands = wavefunctions.shape
    z_points = stacked // 2
    pools = lax.axis_size("pool")
    groups = lax.axis_size("ga")
    cores = lax.axis_size("pert")
    my_pool = lax.axis_index("pool")
    my_core = lax.axis_index("pert")
    my_group = lax.axis_index("ga")
    cap = max(2, local_k // pools + 1)
    half = columns // cores
    share = bands // groups
    ids = jnp.stack([my_pool, my_core, my_group]).astype(jnp.int32)
    waves = wavefunctions.reshape(local_k * cores, half * stacked, bands)
    swap_cores = [(c, cores - 1 - c) for c in range(cores)]

    plan = make_plan(ids, partners, pools, local_k, cap)
    moves, waits = transfers(pools, cap)
    gives = [pick(plan, ids, waves, pools, cap, move) for move in moves]
    potentials = after(potentials, gives[0])

    per_device = potentials.shape[0]
    by_half = potentials.reshape(per_device, cores, half, stacked)
    mine_now = lax.dynamic_index_in_dim(by_half, my_core, 1, keepdims=False)
    theirs_now = lax.dynamic_index_in_dim(by_half, 1 - my_core, 1, keepdims=False)
    other_pots = lax.ppermute(theirs_now, "pert", swap_cores)
    ordered = jnp.roll(pert_order.reshape(cores, per_device), -my_core, axis=0).reshape(-1)
    stored = jnp.where(
        my_core == 0, jnp.stack([mine_now, other_pots]), jnp.stack([other_pots, mine_now])
    ).reshape((cores * per_device,) + mine_now.shape[1:])
    options = jnp.arange(cores * per_device, dtype=jnp.int32)
    chosen = jnp.sum(
        jnp.where(
            (ordered[:, None] == options[None, :])[:, :, None, None], stored[None],
            jnp.zeros((), F32),
        ),
        axis=1,
    ).reshape(cores * per_device, half, 2, z_points)
    pots = jnp.moveaxis(chosen, 2, 1).reshape(cores * per_device, 2, half * z_points, 1)
    pots = jnp.broadcast_to(pots, pots.shape[:3] + (bands,))
    table = dft_table(z_points)
    scaling = 1.0 / math.sqrt(columns * groups * z_points)

    landed = []
    for move, wait, give in zip(moves, waits, gives):
        if wait is not None:
            give = after(give, landed[wait])
        pairs = [(p, (p + move[0]) % pools) for p in range(pools)]
        landed.append(lax.ppermute(give, "pool", pairs))

    chunks = [((0, 0, cap), waves), *zip(moves, landed)]
    kept, got, terms = [], [], []
    result = None

    def exchange(i):
        sent = []
        size = piece_of(kept[i].shape[0])
        for step in range(1, groups):
            rows = slice(step * share, (step + 1) * share)
            pairs = [(g, (g + step) % groups) for g in range(groups)]
            total = jnp.concatenate(
                [
                    kept[i][at * size : at * size + piece.shape[0], :, rows]
                    + piece[:, :, rows].astype(F32)
                    for at, piece in enumerate(got[i])
                ],
                axis=0,
            )
            sent.append(lax.ppermute(total.astype(BF16), "ga", pairs))
        terms.append(sent)

    finished = 0

    def finish(until, result):
        parcels = [(chunks[i][0], kept[i], got[i], terms[i]) for i in range(finished, until)]
        return combine(plan, result, parcels, local_k, pools, cap, scaling)

    last = len(chunks) - 1
    for i, (chunk, other) in enumerate(chunks):
        if i >= 1:
            other = after(other, kept[i - 1])
        if i >= LAG_CORE:
            exchange(i - LAG_CORE)
            other = after(other, *got[i - LAG_CORE])
        if i >= LAG_GROUP:
            other = after(other, *terms[i - LAG_GROUP])
        if last - i in COMBINE and i - LAG_GROUP + 1 > finished:
            result = finish(i - LAG_GROUP + 1, result)
            finished = i - LAG_GROUP + 1
            other = after(other, result)
        if i == 0:
            other = after(other, *gives[2:3])
        keep, *gives_now = couple(plan, ids, table, pots, waves, other, chunk, pools, cap, groups)
        kept.append(keep)
        if i >= last - 1:
            gives_now[-1] = after(gives_now[-1], *terms[i - 1])
        if i == last - 1:
            gives_now[-1] = after(gives_now[-1], landed[-1])
        got.append([lax.ppermute(give, "pert", swap_cores) for give in gives_now])
    for i in range(len(terms), len(chunks)):
        exchange(i)
    result = finish(last, result)
    finished = last
    result = finish(len(chunks), result)
    return result.reshape(local_k, per_device, 2, share, bands)


LAG_CORE, LAG_GROUP = 1, 2
COMBINE = (1,)


def solution(mesh):
    return jax.shard_map(
        body,
        mesh=mesh,
        in_specs=(P("pool", "ga", None, None), P(("pb", "pert"), "ga", None), P(), P("pb")),
        out_specs=P(("pb", "pool"), "pert", None, "ga", None),
        check_vma=False,
    )
```
